512 devices in a mesh: ctx: 32 (over x_hi, z, core), dp: 16 (over y, x_lo).
Axes of the slice: x: 4 (x_hi: 2, x_lo: 2; x = x_hi * 2 + x_lo), y: 8, z: 8, core: 2. Of those that a mesh axis runs over, the one named last changes fastest.
Arguments:
- x_tokens: bfloat16 [16, 4096, 8192], P('dp', 'ctx'), may hold values from -6 to 6
- grad_out: bfloat16 [16, 4096, 8192], P('dp', 'ctx'), may hold values from -0.011962891 to 0.011962891
- step_raw: bfloat16 [16, 4096, 128], P('dp', 'ctx'), may hold values from -5 to 5
- step_bias: float32 [128], P('ctx'), may hold values from -1.5 to 0.5
- decay_log: float32 [128], P('ctx'), may hold values from -20 to -3, as said below
- b_proj: bfloat16 [16, 4096, 512], P('dp', 'ctx'), may hold values from -2.09375 to 2.09375
- c_proj: bfloat16 [16, 4096, 512], P('dp', 'ctx'), may hold values from -2.09375 to 2.09375
Outputs:
- grad_b: float32 [16, 4096, 512], P('dp', 'ctx')
- grad_c: float32 [16, 4096, 512], P('dp', 'ctx')
- grad_step: bfloat16 [16, 4096, 128], P('dp', 'ctx')
- grad_decay: float32 [128], P('ctx')
- grad_bias: float32 [128], P('ctx')
- grad_skip: float32 [128], P('ctx')
The draws below stay inside these ranges and needn't reach their ends.
Inputs may be any that keep to these rules, and one draw needn't show every extreme that they name: Every head's decay rate exp(decay_log) is positive and below 1 / 20.
All inputs are finite; a program needn't handle non-finite values.
Results may differ from the reference program's by a relative error of at most 0.015.
Values may be sent and summed in bfloat16 or wider, within the bound.
A program may use at most 128 MiB of HBM per device.

```python
import math
from functools import partial
import jax
import jax.numpy as jnp
from jax import lax

HEADS = 128
HEADDIM = 64
STATE = 128
GROUPS = 4
BLOCK = 256
TOK_DEV = 128
SEQLEN = 4096
NSEQ = 16
N_CTX = 32


def draw_decay_log(key, part):
    key = jax.random.fold_in(key, 11)
    first = jax.random.fold_in(key, 0)
    values = jax.random.uniform(first, (HEADS,), jnp.float32, math.log(0.5 / SEQLEN), math.log(1.0 / 30.0))
    return values.astype(jnp.float32)


def draw_step_raw(key, part):
    key = jax.random.fold_in(key, 12)
    first, second = jax.random.split(key)
    pieces = SEQLEN // TOK_DEV
    offsets = jax.random.uniform(first, (NSEQ, pieces, 1, HEADS), jnp.float32, -1.0, 1.0)
    noise = jnp.clip(0.7 * jax.random.normal(second, (NSEQ, pieces, TOK_DEV, HEADS), jnp.float32), -3.0, 3.0)
    return (noise + offsets).reshape(NSEQ, SEQLEN, HEADS).astype(jnp.bfloat16)


def steps_of(stream_key, shape, cuts, least, high):
    level = 1.0
    for axis_at, shards_of in cuts:
        draws = jax.random.uniform(jax.random.fold_in(jax.random.fold_in(stream_key, 6), axis_at), (shards_of,), jnp.float32, least / len(cuts), high / len(cuts))
        level = level * jnp.repeat(jnp.exp(draws), shape[axis_at] // shards_of).reshape((-1,) + (1,) * (len(shape) - 1 - axis_at))
    return level


def normal_values(rng, extent, scale, bound, cuts=(), kind=jnp.bfloat16):
    level = steps_of(rng, extent, cuts, -0.22, 0.18) if cuts else 1.0
    array = jax.random.normal(rng, extent, jnp.float32) * scale * level
    return jnp.minimum(jnp.maximum(array, -bound), bound).astype(kind)


def setup_inputs(seed: int = 0) -> dict:
    splits = jax.random.split(jax.random.key(seed), 8)
    x_tokens = normal_values(splits[0], (NSEQ, SEQLEN, HEADS * HEADDIM), 1.0, 6.0, ((0, 16), (1, 32)))
    grad_out = normal_values(splits[1], (NSEQ, SEQLEN, HEADS * HEADDIM), 0.002, 0.011962891, ((0, 16), (1, 32)))
    step_raw = draw_step_raw(jax.random.fold_in(splits[7], 71), 0)
    step_bias = jnp.clip(-1.5 + 2.0 * jax.random.uniform(splits[3], (HEADS,), jnp.float32) ** steps_of(splits[3], (HEADS,), ((0, 32),), -0.2, 0.2), -1.5, 0.5)
    decay_log = draw_decay_log(jax.random.fold_in(splits[7], 71), 0)
    b_proj = normal_values(splits[5], (NSEQ, SEQLEN, GROUPS * STATE), 0.35, 2.09375, ((0, 16), (1, 32)))
    c_proj = normal_values(splits[6], (NSEQ, SEQLEN, GROUPS * STATE), 0.35, 2.09375, ((0, 16), (1, 32)))
    return dict(x_tokens=x_tokens, grad_out=grad_out, step_raw=step_raw, step_bias=step_bias, decay_log=decay_log, b_proj=b_proj, c_proj=c_proj)


def product(form, left, right):
    return jnp.einsum(form, left.astype(jnp.float32), right.astype(jnp.float32))

def block_step(state_in, block_items, decay_rate):
    x_block, step_block, b_block, c_block = block_items
    width = step_block.shape[0]
    b_half = b_block.astype(jnp.bfloat16)
    c_half = c_block.astype(jnp.bfloat16)
    cum_decay = jnp.cumsum(step_block * decay_rate[None, :], axis=0)
    scores = jnp.dot(c_half, b_half.T, preferred_element_type=jnp.float32)
    positions = jnp.arange(width, dtype=jnp.int32)
    causal = positions[:, None] >= positions[None, :]
    gap_sum = jnp.where(causal[:, :, None], cum_decay[:, None, :] - cum_decay[None, :, :], -jnp.inf)
    mixing = (scores[:, :, None] * jnp.exp(gap_sum) * step_block[None, :, :]).astype(jnp.bfloat16)
    inner_part = product('ijh,jhp->ihp', mixing, x_block)
    carried = jnp.einsum('in,hnp->ihp', c_block, state_in, precision=lax.Precision.HIGHEST) * jnp.exp(cum_decay)[:, :, None]
    tail_sum = cum_decay[-1]
    feed_rows = (b_block[:, None, :] * (jnp.exp(tail_sum[None, :] - cum_decay) * step_block)[:, :, None]).astype(jnp.bfloat16)
    fresh_state = product('jhn,jhp->hnp', feed_rows, x_block)
    state_out = jnp.exp(tail_sum)[:, None, None] * state_in + fresh_state
    return (state_out, inner_part + carried)

def local_grads(x_heads, grad_heads, raw_heads, b_rows, c_rows, step_bias, decay_log, block):
    seq_len, head_count = raw_heads.shape
    blocks = seq_len // block

    def objective(raw_value, bias_value, log_value, b_value, c_value):
        step_size = jax.nn.softplus(raw_value + bias_value[None, :])
        decay_rate = -jnp.exp(log_value)
        stepper = jax.checkpoint(partial(block_step, decay_rate=decay_rate))
        start = jnp.zeros((head_count, STATE, HEADDIM), jnp.float32)
        _, outputs = lax.scan(stepper, start, (x_heads.reshape(blocks, block, head_count, HEADDIM), step_size.reshape(blocks, block, head_count), b_value.reshape(blocks, block, STATE), c_value.reshape(blocks, block, STATE)))
        return jnp.sum(outputs * grad_heads.reshape(blocks, block, head_count, HEADDIM).astype(jnp.float32))
    gradients = jax.grad(objective, argnums=(0, 1, 2, 3, 4))(raw_heads.astype(jnp.float32), step_bias, decay_log, b_rows.astype(jnp.float32), c_rows.astype(jnp.float32))
    grad_raw, grad_bias, grad_decay, grad_brows, grad_crows = gradients
    grad_skip = product('lhp,lhp->h', x_heads, grad_heads)
    return (grad_brows.astype(jnp.bfloat16), grad_crows.astype(jnp.bfloat16), grad_raw.astype(jnp.bfloat16), grad_decay, grad_bias, grad_skip)

def reference(x_tokens, grad_out, step_raw, step_bias, decay_log, b_proj, c_proj):
    head_count = HEADS // N_CTX
    repeat = N_CTX // GROUPS

    def one_sequence(seq_items):
        x_seq, grad_seq, raw_seq, b_seq, c_seq = seq_items
        x_split = x_seq.reshape(SEQLEN, N_CTX, head_count, HEADDIM)
        grad_split = grad_seq.reshape(SEQLEN, N_CTX, head_count, HEADDIM)
        raw_split = raw_seq.reshape(SEQLEN, N_CTX, head_count)

        def one_block(block_index):
            x_heads = lax.dynamic_index_in_dim(x_split, block_index, 1, keepdims=False)
            grad_heads = lax.dynamic_index_in_dim(grad_split, block_index, 1, keepdims=False)
            raw_heads = lax.dynamic_index_in_dim(raw_split, block_index, 1, keepdims=False)
            group_index = (block_index // repeat).astype(jnp.int32)
            b_rows = lax.dynamic_slice_in_dim(b_seq, group_index * STATE, STATE, 1)
            c_rows = lax.dynamic_slice_in_dim(c_seq, group_index * STATE, STATE, 1)
            bias_here = lax.dynamic_slice_in_dim(step_bias, (block_index * head_count).astype(jnp.int32), head_count, 0)
            log_here = lax.dynamic_slice_in_dim(decay_log, (block_index * head_count).astype(jnp.int32), head_count, 0)
            return local_grads(x_heads, grad_heads, raw_heads, b_rows, c_rows, bias_here, log_here, BLOCK)
        return lax.map(one_block, jnp.arange(N_CTX, dtype=jnp.int32))
    results = lax.map(one_sequence, (x_tokens, grad_out, step_raw, b_proj, c_proj))
    part_b, part_c, part_step, part_decay, part_bias, part_skip = results
    grad_b = part_b.astype(jnp.float32).reshape(NSEQ, GROUPS, repeat, SEQLEN, STATE).sum(axis=2)
    grad_b = grad_b.transpose(0, 2, 1, 3).reshape(NSEQ, SEQLEN, GROUPS * STATE)
    grad_c = part_c.astype(jnp.float32).reshape(NSEQ, GROUPS, repeat, SEQLEN, STATE).sum(axis=2)
    grad_c = grad_c.transpose(0, 2, 1, 3).reshape(NSEQ, SEQLEN, GROUPS * STATE)
    grad_step = part_step.transpose(0, 2, 1, 3).reshape(NSEQ, SEQLEN, HEADS)
    grad_decay = part_decay.sum(axis=0).reshape(HEADS)
    grad_bias = part_bias.sum(axis=0).reshape(HEADS)
    grad_skip = part_skip.sum(axis=0).reshape(HEADS)
    return (grad_b, grad_c, grad_step, grad_decay, grad_bias, grad_skip)
```

```python
from functools import partial

import jax
import jax.numpy as jnp
from jax import lax
from jax.experimental import pallas as pl
from jax.experimental.pallas import tpu as pltpu
from jax.sharding import PartitionSpec as P

HEADDIM = 64
STATE = 128
LANES = 128
WIDE = 512
SKEW = 5
F32 = jnp.float32
BF16 = jnp.bfloat16
MESH = pl.DeviceIdType.MESH


def mm(a, b):
    return lax.dot_general(a, b, (((1,), (0,)), ((), ())), preferred_element_type=F32)


def mm_nt(a, b):
    return lax.dot_general(a, b, (((1,), (1,)), ((), ())), preferred_element_type=F32)


def mm_exact(a, b):
    return lax.dot_general(
        a, b, (((1,), (0,)), ((), ())), precision=lax.Precision.HIGHEST, preferred_element_type=F32
    )


def halves(v):
    high = v.astype(BF16)
    return high, (v - high.astype(F32)).astype(BF16)


def pack(v):
    return (v * jnp.abs(v)).astype(BF16)


def unpack(code):
    u = code.astype(F32)
    root = jnp.sqrt(jnp.abs(u))
    return jnp.where(u < 0.0, -root, root)


def kernel(
    chips, copies_dp, x, g, b, c, raw, par,
    gb, gc, gs, gp,
    xs, gr, bs, cs, rs,
    eh, fh, eg, fx, eg_low, fx_low, fresh, back, s_in, t_in, send_f, send_b, recv_f, recv_b, scale,
    gram, mix, mixt, bt, ct, row, col, dcs, dbs, skip_l, tail_l, draw_s, draw_r,
    par_r, sum_s, sum_r, all_s, all_r,
    own_sem, pair_send, pair_recv, fs_sem, fr_sem, bs_sem, br_sem, out_send, out_recv,
    ps_sem, pr_sem, ss_sem, sr_sem, as_sem, ar_sem,
):
    me = lax.axis_index("ctx")
    me_dp = lax.axis_index("dp")
    core = lax.rem(me, 2)
    pos = lax.div(me, 2)
    count = 2 * chips
    partner = me + 1 - 2 * core
    after = lax.rem(me + 2, count)
    before = lax.rem(me + count - 2, count)
    tok = x.shape[0]
    rows = 2 * tok
    half = xs.shape[1]
    cols = bs.shape[1]
    groups = cols // STATE
    steps = half // WIDE
    per_group = steps // groups
    heads_w = WIDE // HEADDIM
    pieces = half // LANES
    sub = WIDE // LANES
    first_head = core * (half // HEADDIM)
    my_half = lax.div(me, chips)
    my_place = lax.rem(me, chips)

    mine_rows = pl.ds(pl.multiple_of(core * tok, tok), tok)
    their_rows = pl.ds(pl.multiple_of((1 - core) * tok, tok), tok)
    mine_b = pl.ds(pl.multiple_of(core * cols, cols), cols)
    their_b = pl.ds(pl.multiple_of((1 - core) * cols, cols), cols)

    def lanes_of(q):
        return pl.ds(pl.multiple_of(q * WIDE, WIDE), WIDE)

    def moves_of(q):
        mine = pl.ds(pl.multiple_of(core * half + q * WIDE, WIDE), WIDE)
        theirs = pl.ds(pl.multiple_of((1 - core) * half + q * WIDE, WIDE), WIDE)
        return [
            (x.at[:, mine], x.at[:, theirs], xs.at[mine_rows, lanes_of(q)], 3 + 2 * q),
            (g.at[:, mine], g.at[:, theirs], gr.at[mine_rows, lanes_of(q)], 4 + 2 * q),
        ]

    small_moves = [
        (raw, raw, rs.at[mine_rows], 0),
        (b.at[:, mine_b], b.at[:, their_b], bs.at[mine_rows], 1),
        (c.at[:, mine_b], c.at[:, their_b], cs.at[mine_rows], 2),
    ]

    def own_copy(move):
        return pltpu.make_async_copy(move[0], move[2], own_sem.at[move[3]])

    def pair_copy(move):
        return pltpu.make_async_remote_copy(
            src_ref=move[1], dst_ref=move[2],
            send_sem=pair_send.at[move[3]], recv_sem=pair_recv.at[move[3]],
            device_id={"ctx": partner}, device_id_type=MESH,
        )

    for move in small_moves:
        own_copy(move).start()

    def start_own(q, carry):
        for move in moves_of(q):
            own_copy(move).start()
        return carry

    lax.fori_loop(0, steps, start_own, 0)

    barrier = pltpu.get_barrier_semaphore()

    def greet(d, carry):
        pl.semaphore_signal(
            barrier, inc=1, device_id={"ctx": lax.rem(me + d, count)}, device_id_type=MESH
        )
        return carry

    def greet_dp(d, carry):
        pl.semaphore_signal(
            barrier, inc=1, device_id={"dp": lax.rem(me_dp + d, copies_dp)}, device_id_type=MESH
        )
        return carry

    lax.fori_loop(1, count, greet, 0)
    lax.fori_loop(1, copies_dp, greet_dp, 0)
    pl.semaphore_wait(barrier, count - 1 + copies_dp - 1)

    def par_copy(j, place):
        return pltpu.make_async_remote_copy(
            src_ref=par, dst_ref=par_r.at[place], send_sem=ps_sem.at[j], recv_sem=pr_sem.at[place],
            device_id={"ctx": 2 * j + my_half}, device_id_type=MESH,
        )

    def par_send(j, carry):
        @pl.when(2 * j + my_half != me)
        def _():
            par_copy(j, my_place).start()

        return carry

    lax.fori_loop(0, chips, par_send, 0)

    for move in small_moves:
        pair_copy(move).start()

    def start_pair(q, carry):
        for move in moves_of(q):
            pair_copy(move).start()
        return carry

    lax.fori_loop(0, steps, start_pair, 0)

    gram[...] = jnp.zeros_like(gram)
    row[...] = jnp.zeros_like(row)
    col[...] = jnp.zeros_like(col)
    dcs[...] = jnp.zeros_like(dcs)
    dbs[...] = jnp.zeros_like(dbs)

    @pl.when(pos == 0)
    def _():
        recv_f[...] = jnp.zeros_like(recv_f)

    @pl.when(pos == chips - 1)
    def _():
        recv_b[...] = jnp.zeros_like(recv_b)

    for move in small_moves:
        own_copy(move).wait()
        pair_copy(move).wait()

    i_at = lax.broadcasted_iota(jnp.int32, (rows, rows), 0)
    j_at = lax.broadcasted_iota(jnp.int32, (rows, rows), 1)
    causal = i_at >= j_at
    for at in range(groups):
        span = slice(at * STATE, (at + 1) * STATE)
        b_at = bs[:, span]
        c_at = cs[:, span]
        bt[at] = b_at.astype(F32).T.astype(BF16)
        ct[at] = c_at.astype(F32).T.astype(BF16)
        scores = jnp.where(causal, mm_nt(c_at, b_at), 0.0)
        mix[at] = scores.astype(BF16)
        mixt[at] = scores.T.astype(BF16)

    @pl.when(my_half == core)
    def _():
        par_r[my_place] = par[...]

    def par_wait(j, carry):
        @pl.when(chips * core + j != me)
        def _():
            par_copy(j, j).wait_recv()

        return carry

    lax.fori_loop(0, chips, par_wait, 0)

    def step_sizes():
        params = jnp.sum(par_r[...], axis=0)
        z = rs[...].astype(F32) + params[0:1, :]
        dt = jnp.maximum(z, 0.0) + jnp.log1p(jnp.exp(-jnp.abs(z)))
        lane = lax.broadcasted_iota(jnp.int32, (1, z.shape[1]), 1)
        own = lax.div(lane, z.shape[1] // 2) == core
        return z, dt, jnp.where(own, -jnp.exp(params[1:2, :]), 0.0)

    z, dt, rate = step_sizes()
    cum = mm_exact(causal.astype(F32), dt * rate)
    mid = cum[rows - 1 : rows, :] * 0.5
    e_hi, e_lo = halves(jnp.exp(cum - mid))
    f_hi, f_lo = halves(jnp.exp(mid - cum) * dt)
    eh[:, :LANES] = e_hi
    eh[:, LANES:] = e_lo
    fh[:, :LANES] = f_hi
    fh[:, LANES:] = f_lo
    a_hi, a_lo = halves(jnp.broadcast_to(jnp.exp(mid), (16, LANES)))
    a_both = jnp.concatenate([a_hi, a_lo], axis=1)

    def spread_of(q):
        head = lax.broadcasted_iota(jnp.int32, (LANES, WIDE), 0)
        lane = lax.broadcasted_iota(jnp.int32, (LANES, WIDE), 1)
        return (head == first_head + q * heads_w + lax.div(lane, HEADDIM)).astype(F32).astype(BF16)

    def fold(v, spread):
        high, low = halves(v)
        return mm_nt(high, spread) + mm_nt(low, spread)

    def full(high, low, here):
        return high[:, here].astype(F32) + low[:, here].astype(F32)

    def dense(q):
        for move in moves_of(q):
            own_copy(move).wait()
            pair_copy(move).wait()
        at = lax.div(q, per_group)
        here = lanes_of(q)
        spread = spread_of(q)
        both = jnp.concatenate([spread, spread], axis=0)
        x_q = xs[:, here].astype(F32)
        g_q = gr[:, here].astype(F32)
        skip_l[0:1, here] = jnp.sum(x_q * g_q, axis=0, keepdims=True)
        eg_q, eg_rest = halves(mm(eh[...], both) * g_q)
        fx_q, fx_rest = halves(mm(fh[...], both) * x_q)
        eg[:, here] = eg_q
        fx[:, here] = fx_q
        eg_low[:, here] = eg_rest
        fx_low[:, here] = fx_rest
        fresh_q = mm(bt[at], fx_q) + mm(bt[at], fx_rest)
        back_q = mm(ct[at], eg_q) + mm(ct[at], eg_rest)
        scale_q = mm(a_both, both)
        for k in range(sub):
            span = slice(k * LANES, (k + 1) * LANES)
            fresh[q * sub + k] = fresh_q[:, span]
            back[q * sub + k] = back_q[:, span]
            scale[q * sub + k] = scale_q[0:8, span]

    def inner(q):
        at = lax.div(q, per_group)
        here = lanes_of(q)
        spread = spread_of(q)
        eg_q = eg[:, here]
        fx_q = fx[:, here]
        gram[at] += mm_nt(eg_q, fx_q)
        y_q = mm(mix[at], fx_q) + mm(mix[at], fx_low[:, here])
        v_q = mm(mixt[at], eg_q) + mm(mixt[at], eg_low[:, here])
        row[...] += fold(full(eg, eg_low, here) * y_q, spread)
        col[...] += fold(full(fx, fx_low, here) * v_q, spread)

    def cross():
        for at in range(groups):
            span = slice(at * STATE, (at + 1) * STATE)
            cot = jnp.where(causal, gram[at], 0.0)
            dcs[:, span] += mm(cot.astype(BF16), bs[:, span])
            dbs[:, span] += mm(cot.T.astype(BF16), cs[:, span])

    def outer(q):
        at = lax.div(q, per_group)
        here = lanes_of(q)
        span = pl.ds(pl.multiple_of(at * STATE, STATE), STATE)
        spread = spread_of(q)
        s_q = jnp.concatenate([s_in[q * sub + k] for k in range(sub)], axis=1)
        t_q = jnp.concatenate([t_in[q * sub + k] for k in range(sub)], axis=1)
        f_q = jnp.concatenate([fresh[q * sub + k] for k in range(sub)], axis=1)
        row[...] += fold(full(eg, eg_low, here) * mm(cs[:, span], s_q), spread)
        col[...] += fold(full(fx, fx_low, here) * mm(bs[:, span], t_q), spread)
        dcs[:, span] += mm_nt(eg[:, here], s_q)
        dbs[:, span] += mm_nt(fx[:, here], t_q)
        whole = (s_q.astype(F32) + f_q) * t_q.astype(F32)
        tail_l[0:1, here] = jnp.sum(whole, axis=0, keepdims=True)

    def up(k):
        return pltpu.make_async_remote_copy(
            src_ref=send_f.at[k], dst_ref=recv_f.at[k], send_sem=fs_sem.at[k], recv_sem=fr_sem.at[k],
            device_id={"ctx": after}, device_id_type=MESH,
        )

    def down(k):
        return pltpu.make_async_remote_copy(
            src_ref=send_b.at[k], dst_ref=recv_b.at[k], send_sem=bs_sem.at[k], recv_sem=br_sem.at[k],
            device_id={"ctx": before}, device_id_type=MESH,
        )

    far = (chips - 1) * SKEW
    near = jnp.minimum(pos, chips - 1 - pos)
    inner_from = jnp.where(near >= chips // 4, 2, near * SKEW + pieces)
    inner_from = jnp.minimum(inner_from, far + sub - 1)

    def slot(t, carry):
        k_f = t - pos * SKEW
        k_b = t - (chips - 1 - pos) * SKEW

        @pl.when((t < sub * steps) & (lax.rem(t, sub) == 0))
        def _():
            dense(lax.div(t, sub))

        @pl.when((k_f >= 0) & (k_f < pieces))
        def _():
            @pl.when(pos > 0)
            def _():
                up(k_f).wait_recv()

            by = scale[k_f][0:1, :]
            entering = by * unpack(recv_f[k_f])
            s_in[k_f] = entering.astype(BF16)

            @pl.when(pos < chips - 1)
            def _():
                send_f[k_f] = pack(by * (entering + fresh[k_f]))
                up(k_f).start()

        @pl.when((k_b >= 0) & (k_b < pieces))
        def _():
            @pl.when(pos < chips - 1)
            def _():
                down(k_b).wait_recv()

            by = scale[k_b][0:1, :]
            entering = by * unpack(recv_b[k_b])
            t_in[k_b] = entering.astype(BF16)

            @pl.when(pos > 0)
            def _():
                send_b[k_b] = pack(by * (entering + back[k_b]))
                down(k_b).start()

        k_i = t - inner_from

        @pl.when((k_i >= 0) & (k_i < sub * steps) & (lax.rem(k_i, sub) == 0))
        def _():
            inner(lax.div(k_i, sub))

        @pl.when(k_i == sub * steps)
        def _():
            cross()

        k_o = t - far - sub

        @pl.when((k_o >= 0) & (lax.rem(k_o, sub) == 0))
        def _():
            outer(lax.div(k_o, sub))

        return carry

    lax.fori_loop(0, far + sub + pieces, slot, 0)

    def gather_rows(q, carry):
        spread = spread_of(q)
        here = lanes_of(q)
        tail_q = fold(jnp.broadcast_to(tail_l[0:1, here], (16, WIDE)), spread)
        skip_q = fold(jnp.broadcast_to(skip_l[0:1, here], (16, WIDE)), spread)
        return (carry[0] + tail_q[0:1, :], carry[1] + skip_q[0:1, :])

    zero = jnp.zeros((1, LANES), F32)
    d_tail, d_skip = lax.fori_loop(0, steps, gather_rows, (zero, zero))

    z, dt, rate = step_sizes()
    d_a = d_tail + mm_exact((i_at <= j_at).astype(F32), row[...] - col[...])
    d_dt = col[...] / dt + rate * d_a
    d_raw = d_dt * jax.nn.sigmoid(z)
    sum_s[...] = jnp.zeros_like(sum_s)
    sum_s[0:1, :] = rate * jnp.sum(d_a * dt, axis=0, keepdims=True)
    sum_s[1:2, :] = jnp.sum(d_raw, axis=0, keepdims=True)
    sum_s[2:3, :] = d_skip
    draw_s[...] = d_raw

    def sum_copy(j, place):
        return pltpu.make_async_remote_copy(
            src_ref=sum_s, dst_ref=sum_r.at[place], send_sem=ss_sem.at[j], recv_sem=sr_sem.at[place],
            device_id={"ctx": chips * core + j}, device_id_type=MESH,
        )

    def sum_send(j, carry):
        @pl.when(chips * core + j != me)
        def _():
            sum_copy(j, pos).start()

        return carry

    lax.fori_loop(0, chips, sum_send, 0)

    backs = [
        (dbs.at[their_rows], gb.at[:, mine_b]),
        (dcs.at[their_rows], gc.at[:, mine_b]),
        (draw_s.at[their_rows], draw_r),
    ]
    copies = []
    for at, (src, dst) in enumerate(backs):
        copy = pltpu.make_async_remote_copy(
            src_ref=src, dst_ref=dst, send_sem=out_send.at[at], recv_sem=out_recv.at[at],
            device_id={"ctx": partner}, device_id_type=MESH,
        )
        copy.start()
        copies.append(copy)
    gb[:, mine_b] = dbs[mine_rows, :]
    gc[:, mine_b] = dcs[mine_rows, :]

    @pl.when(my_half == core)
    def _():
        sum_r[pos] = sum_s[...]

    def sum_wait(j, carry):
        @pl.when(2 * j + my_half != me)
        def _():
            sum_copy(j, j).wait_recv()

        return carry

    lax.fori_loop(0, chips, sum_wait, 0)
    total = jnp.sum(sum_r[...], axis=0)
    all_s[...] = total

    def all_copy(d, place):
        return pltpu.make_async_remote_copy(
            src_ref=all_s, dst_ref=all_r.at[place], send_sem=as_sem.at[d], recv_sem=ar_sem.at[place],
            device_id={"dp": lax.rem(me_dp + d, copies_dp)}, device_id_type=MESH,
        )

    def all_send(d, carry):
        all_copy(d, d).start()
        return carry

    def all_wait(d, carry):
        all_copy(d, d).wait()
        return carry

    lax.fori_loop(1, copies_dp, all_send, 0)

    def drain(k, carry):
        @pl.when(pos < chips - 1)
        def _():
            up(k).wait_send()

        @pl.when(pos > 0)
        def _():
            down(k).wait_send()

        return carry

    lax.fori_loop(0, pieces, drain, 0)

    def drain_small(j, carry):
        @pl.when(2 * j + my_half != me)
        def _():
            par_copy(j, my_place).wait_send()

        @pl.when(chips * core + j != me)
        def _():
            sum_copy(j, pos).wait_send()

        return carry

    lax.fori_loop(0, chips, drain_small, 0)
    for copy in copies:
        copy.wait()
    gs[...] = (draw_s[mine_rows, :] + draw_r[...]).astype(BF16)
    lax.fori_loop(1, copies_dp, all_wait, 0)
    all_r[0] = total
    heads = total.shape[1]
    span = heads // count
    head = lax.broadcasted_iota(jnp.int32, (heads, heads), 0)
    lane = lax.broadcasted_iota(jnp.int32, (heads, heads), 1)
    pick = ((head == me * span + lane) & (lane < span)).astype(F32)
    gp[...] = mm_exact(jnp.sum(all_r[...], axis=0), pick)


def run(x, g, b, c, raw, par, chips, copies_dp):
    tok, wide = x.shape
    half = wide // 2
    cols = b.shape[1] // 2
    groups = cols // STATE
    rows = 2 * tok
    pieces = half // LANES
    heads = raw.shape[1]
    steps = half // WIDE
    anywhere = pl.BlockSpec(memory_space=pl.ANY)
    inside = pl.BlockSpec(memory_space=pltpu.VMEM)
    state16 = pltpu.VMEM((pieces, STATE, LANES), BF16)
    state32 = pltpu.VMEM((pieces, STATE, LANES), F32)
    wide16 = pltpu.VMEM((rows, half), BF16)
    tile = pltpu.VMEM((8, heads), F32)
    dma = pltpu.SemaphoreType.DMA
    moves = 3 + 2 * steps
    return pl.pallas_call(
        partial(kernel, chips, copies_dp),
        out_shape=(
            jax.ShapeDtypeStruct((tok, 2 * cols), F32),
            jax.ShapeDtypeStruct((tok, 2 * cols), F32),
            jax.ShapeDtypeStruct((tok, heads), BF16),
            jax.ShapeDtypeStruct((8, heads), F32),
        ),
        in_specs=[anywhere] * 5 + [inside],
        out_specs=(inside,) * 4,
        scratch_shapes=[
            wide16, wide16,
            pltpu.VMEM((rows, cols), BF16), pltpu.VMEM((rows, cols), BF16),
            pltpu.VMEM((rows, heads), BF16),
            pltpu.VMEM((rows, 2 * LANES), BF16), pltpu.VMEM((rows, 2 * LANES), BF16),
            wide16, wide16, wide16, wide16,
            state32, state32, state16, state16, state16, state16, state16, state16,
            pltpu.VMEM((pieces, 8, LANES), F32),
            pltpu.VMEM((groups, rows, rows), F32),
            pltpu.VMEM((groups, rows, rows), BF16), pltpu.VMEM((groups, rows, rows), BF16),
            pltpu.VMEM((groups, STATE, rows), BF16), pltpu.VMEM((groups, STATE, rows), BF16),
            pltpu.VMEM((rows, LANES), F32), pltpu.VMEM((rows, LANES), F32),
            pltpu.VMEM((rows, cols), F32), pltpu.VMEM((rows, cols), F32),
            pltpu.VMEM((8, half), F32), pltpu.VMEM((8, half), F32),
            pltpu.VMEM((rows, heads), F32), pltpu.VMEM((tok, heads), F32),
            pltpu.VMEM((chips, 8, heads), F32),
            tile, pltpu.VMEM((chips, 8, heads), F32),
            tile, pltpu.VMEM((copies_dp, 8, heads), F32),
            dma((moves,)), dma((moves,)), dma((moves,)),
            dma((pieces,)), dma((pieces,)), dma((pieces,)), dma((pieces,)),
            dma((3,)), dma((3,)),
            dma((chips,)), dma((chips,)), dma((chips,)), dma((chips,)),
            dma((copies_dp,)), dma((copies_dp,)),
        ],
        compiler_params=pltpu.CompilerParams(
            collective_id=0, has_side_effects=True, vmem_limit_bytes=60 * 1024 * 1024
        ),
        name="scan_backward",
    )(x, g, b, c, raw, par)


def local(x_tokens, grad_out, step_raw, step_bias, decay_log, b_proj, c_proj):
    shards = lax.axis_size("ctx")
    me = lax.axis_index("ctx")
    span = step_bias.shape[0]
    mine = lax.broadcasted_iota(jnp.int32, (8, span * shards), 1) // span == me
    pair = jnp.tile(jnp.stack([step_bias, decay_log]), (4, shards))
    par = jnp.where(mine, pair, 0.0)
    gb, gc, gs, gp = run(
        x_tokens[0], grad_out[0], b_proj[0], c_proj[0], step_raw[0], par,
        shards // 2, lax.axis_size("dp"),
    )
    return (gb[None], gc[None], gs[None], gp[0, :span], gp[1, :span], gp[2, :span])


def solution(mesh):
    tokens = P("dp", "ctx", None)
    return jax.shard_map(
        local,
        mesh=mesh,
        in_specs=(tokens, tokens, tokens, P("ctx"), P("ctx"), tokens, tokens),
        out_specs=(tokens, tokens, tokens, P("ctx"), P("ctx"), P("ctx")),
        check_vma=False,
    )
```

```python
from functools import partial

import jax
import jax.numpy as jnp
from jax import lax
from jax.experimental import pallas as pl
from jax.experimental.pallas import tpu as pltpu
from jax.sharding import PartitionSpec as P

HEADDIM = 64
STATE = 128
LANES = 128
WIDE = 512
SKEW = 7
F32 = jnp.float32
BF16 = jnp.bfloat16
MESH = pl.DeviceIdType.MESH


def mm(a, b):
    return lax.dot_general(a, b, (((1,), (0,)), ((), ())), preferred_element_type=F32)


def mm_nt(a, b):
    return lax.dot_general(a, b, (((1,), (1,)), ((), ())), preferred_element_type=F32)


def mm_exact(a, b):
    return lax.dot_general(
        a, b, (((1,), (0,)), ((), ())), precision=lax.Precision.HIGHEST, preferred_element_type=F32
    )


def halves(v):
    high = v.astype(BF16)
    return high, (v - high.astype(F32)).astype(BF16)


def pack(v):
    return (v * jnp.abs(v)).astype(BF16)


def unpack(code):
    u = code.astype(F32)
    root = jnp.sqrt(jnp.abs(u))
    return jnp.where(u < 0.0, -root, root)


def kernel(
    chips, copies_dp, x, g, b, c, raw, bias, log_rate,
    gb, gc, gs, gp,
    xs, gr, bs, cs, rs,
    eh, fh, eg, fx, eg_low, fx_low, fresh, back, s_in, t_in, send_f, send_b, recv_f, recv_b, scale,
    gram, mix, mixt, bt, ct, row, col, dcs, dbs, d_skip, d_tail, draw_s, draw_r,
    par, par_r, sum_s, sum_r, all_s, all_r,
    own_sem, pair_send, pair_recv, fs_sem, fr_sem, bs_sem, br_sem, out_send, out_recv,
    ps_sem, pr_sem, ss_sem, sr_sem, as_sem, ar_sem,
):
    me = lax.axis_index("ctx")
    me_dp = lax.axis_index("dp")
    core = lax.rem(me, 2)
    pos = lax.div(me, 2)
    count = 2 * chips
    partner = me + 1 - 2 * core
    after = lax.rem(me + 2, count)
    before = lax.rem(me + count - 2, count)
    tok = x.shape[0]
    rows = 2 * tok
    half = xs.shape[1]
    cols = bs.shape[1]
    groups = cols // STATE
    steps = half // WIDE
    per_group = steps // groups
    heads_w = WIDE // HEADDIM
    pieces = half // LANES
    sub = WIDE // LANES
    first_head = core * (half // HEADDIM)
    my_half = lax.div(me, chips)
    my_place = lax.rem(me, chips)

    mine_rows = pl.ds(pl.multiple_of(core * tok, tok), tok)
    their_rows = pl.ds(pl.multiple_of((1 - core) * tok, tok), tok)
    mine_b = pl.ds(pl.multiple_of(core * cols, cols), cols)
    their_b = pl.ds(pl.multiple_of((1 - core) * cols, cols), cols)

    def lanes_of(q):
        return pl.ds(pl.multiple_of(q * WIDE, WIDE), WIDE)

    def moves_of(q):
        mine = pl.ds(pl.multiple_of(core * half + q * WIDE, WIDE), WIDE)
        theirs = pl.ds(pl.multiple_of((1 - core) * half + q * WIDE, WIDE), WIDE)
        return [
            (x.at[:, mine], x.at[:, theirs], xs.at[mine_rows, lanes_of(q)], 3 + 2 * q),
            (g.at[:, mine], g.at[:, theirs], gr.at[mine_rows, lanes_of(q)], 4 + 2 * q),
        ]

    small_moves = [
        (raw, raw, rs.at[mine_rows], 0),
        (b.at[:, mine_b], b.at[:, their_b], bs.at[mine_rows], 1),
        (c.at[:, mine_b], c.at[:, their_b], cs.at[mine_rows], 2),
    ]

    def own_copy(move):
        return pltpu.make_async_copy(move[0], move[2], own_sem.at[move[3]])

    def pair_copy(move):
        return pltpu.make_async_remote_copy(
            src_ref=move[1], dst_ref=move[2],
            send_sem=pair_send.at[move[3]], recv_sem=pair_recv.at[move[3]],
            device_id={"ctx": partner}, device_id_type=MESH,
        )

    held = bias.shape[0]
    lane = lax.broadcasted_iota(jnp.int32, (8, par.shape[1]), 1)
    line = lax.broadcasted_iota(jnp.int32, (8, par.shape[1]), 0)
    tile = jnp.zeros(par.shape, F32)
    for k in range(held):
        here = lane == me * held + k
        tile = jnp.where(here & (line == 0), bias[k], tile)
        tile = jnp.where(here & (line == 1), log_rate[k], tile)
    par[...] = tile

    for move in small_moves:
        own_copy(move).start()

    def start_own(q, carry):
        for move in moves_of(q):
            own_copy(move).start()
        return carry

    lax.fori_loop(0, steps, start_own, 0)

    barrier = pltpu.get_barrier_semaphore()

    def greet(d, carry):
        pl.semaphore_signal(
            barrier, inc=1, device_id={"ctx": lax.rem(me + d, count)}, device_id_type=MESH
        )
        return carry

    def greet_dp(d, carry):
        pl.semaphore_signal(
            barrier, inc=1, device_id={"dp": lax.rem(me_dp + d, copies_dp)}, device_id_type=MESH
        )
        return carry

    lax.fori_loop(1, count, greet, 0)
    lax.fori_loop(1, copies_dp, greet_dp, 0)
    pl.semaphore_wait(barrier, count - 1 + copies_dp - 1)

    def par_copy(j, place):
        return pltpu.make_async_remote_copy(
            src_ref=par, dst_ref=par_r.at[place], send_sem=ps_sem.at[j], recv_sem=pr_sem.at[place],
            device_id={"ctx": 2 * j + my_half}, device_id_type=MESH,
        )

    def par_send(j, carry):
        @pl.when(2 * j + my_half != me)
        def _():
            par_copy(j, my_place).start()

        return carry

    lax.fori_loop(0, chips, par_send, 0)

    for move in small_moves:
        pair_copy(move).start()

    def start_pair(q, carry):
        for move in moves_of(q):
            pair_copy(move).start()
        return carry

    lax.fori_loop(0, steps, start_pair, 0)

    gram[...] = jnp.zeros_like(gram)
    row[...] = jnp.zeros_like(row)
    col[...] = jnp.zeros_like(col)
    dcs[...] = jnp.zeros_like(dcs)
    dbs[...] = jnp.zeros_like(dbs)
    d_skip[...] = jnp.zeros_like(d_skip)
    d_tail[...] = jnp.zeros_like(d_tail)

    @pl.when(pos == 0)
    def _():
        recv_f[...] = jnp.zeros_like(recv_f)

    @pl.when(pos == chips - 1)
    def _():
        recv_b[...] = jnp.zeros_like(recv_b)

    for move in small_moves:
        own_copy(move).wait()
        pair_copy(move).wait()

    i_at = lax.broadcasted_iota(jnp.int32, (rows, rows), 0)
    j_at = lax.broadcasted_iota(jnp.int32, (rows, rows), 1)
    causal = i_at >= j_at
    for at in range(groups):
        span = slice(at * STATE, (at + 1) * STATE)
        b_at = bs[:, span]
        c_at = cs[:, span]
        bt[at] = b_at.astype(F32).T.astype(BF16)
        ct[at] = c_at.astype(F32).T.astype(BF16)
        scores = jnp.where(causal, mm_nt(c_at, b_at), 0.0)
        mix[at] = scores.astype(BF16)
        mixt[at] = scores.T.astype(BF16)

    @pl.when(my_half == core)
    def _():
        par_r[my_place] = par[...]

    def par_wait(j, carry):
        @pl.when(chips * core + j != me)
        def _():
            par_copy(j, j).wait_recv()

        return carry

    lax.fori_loop(0, chips, par_wait, 0)

    def step_sizes():
        params = jnp.sum(par_r[...], axis=0)
        z = rs[...].astype(F32) + params[0:1, :]
        dt = jnp.maximum(z, 0.0) + jnp.log1p(jnp.exp(-jnp.abs(z)))
        lane = lax.broadcasted_iota(jnp.int32, (1, z.shape[1]), 1)
        own = lax.div(lane, z.shape[1] // 2) == core
        return z, dt, jnp.where(own, -jnp.exp(params[1:2, :]), 0.0)

    z, dt, rate = step_sizes()
    cum = mm_exact(causal.astype(F32), dt * rate)
    mid = cum[rows - 1 : rows, :] * 0.5
    e_hi, e_lo = halves(jnp.exp(cum - mid))
    f_hi, f_lo = halves(jnp.exp(mid - cum) * dt)
    eh[:, :LANES] = e_hi
    eh[:, LANES:] = e_lo
    fh[:, :LANES] = f_hi
    fh[:, LANES:] = f_lo
    a_hi, a_lo = halves(jnp.broadcast_to(jnp.exp(mid), (16, LANES)))
    a_both = jnp.concatenate([a_hi, a_lo], axis=1)

    def spread_of(q):
        head = lax.broadcasted_iota(jnp.int32, (LANES, WIDE), 0)
        lane = lax.broadcasted_iota(jnp.int32, (LANES, WIDE), 1)
        return (head == first_head + q * heads_w + lax.div(lane, HEADDIM)).astype(F32).astype(BF16)

    def fold(v, spread):
        high, low = halves(v)
        return mm_nt(high, spread) + mm_nt(low, spread)

    def fold_line(v, spread):
        return fold(jnp.broadcast_to(v, (16, WIDE)), spread)[0:8, :]

    def full(high, low, here):
        return high[:, here].astype(F32) + low[:, here].astype(F32)

    def dense(q):
        for move in moves_of(q):
            own_copy(move).wait()
            pair_copy(move).wait()
        at = lax.div(q, per_group)
        here = lanes_of(q)
        spread = spread_of(q)
        both = jnp.concatenate([spread, spread], axis=0)
        x_q = xs[:, here].astype(F32)
        g_q = gr[:, here].astype(F32)
        d_skip[...] += fold_line(jnp.sum(x_q * g_q, axis=0, keepdims=True), spread)
        eg_q, eg_rest = halves(mm(eh[...], both) * g_q)
        fx_q, fx_rest = halves(mm(fh[...], both) * x_q)
        eg[:, here] = eg_q
        fx[:, here] = fx_q
        eg_low[:, here] = eg_rest
        fx_low[:, here] = fx_rest
        fresh_q = mm(bt[at], fx_q) + mm(bt[at], fx_rest)
        back_q = mm(ct[at], eg_q) + mm(ct[at], eg_rest)
        scale_q = mm(a_both, both)
        for k in range(sub):
            span = slice(k * LANES, (k + 1) * LANES)
            fresh[q * sub + k] = fresh_q[:, span]
            back[q * sub + k] = back_q[:, span]
            scale[q * sub + k] = scale_q[0:8, span]

    def inner(q):
        at = lax.div(q, per_group)
        here = lanes_of(q)
        spread = spread_of(q)
        eg_q = eg[:, here]
        fx_q = fx[:, here]
        gram[at] += mm_nt(eg_q, fx_q)
        y_q = mm(mix[at], fx_q) + mm(mix[at], fx_low[:, here])
        v_q = mm(mixt[at], eg_q) + mm(mixt[at], eg_low[:, here])
        row[...] += fold(full(eg, eg_low, here) * y_q, spread)
        col[...] += fold(full(fx, fx_low, here) * v_q, spread)

    def cross():
        for at in range(groups):
            span = slice(at * STATE, (at + 1) * STATE)
            cot = jnp.where(causal, gram[at], 0.0)
            dcs[:, span] += mm(cot.astype(BF16), bs[:, span])
            dbs[:, span] += mm(cot.T.astype(BF16), cs[:, span])

    def outer(q):
        at = lax.div(q, per_group)
        here = lanes_of(q)
        span = pl.ds(pl.multiple_of(at * STATE, STATE), STATE)
        spread = spread_of(q)
        s_q = jnp.concatenate([s_in[q * sub + k] for k in range(sub)], axis=1)
        t_q = jnp.concatenate([t_in[q * sub + k] for k in range(sub)], axis=1)
        f_q = jnp.concatenate([fresh[q * sub + k] for k in range(sub)], axis=1)
        row[...] += fold(full(eg, eg_low, here) * mm(cs[:, span], s_q), spread)
        col[...] += fold(full(fx, fx_low, here) * mm(bs[:, span], t_q), spread)
        dcs[:, span] += mm_nt(eg[:, here], s_q)
        dbs[:, span] += mm_nt(fx[:, here], t_q)
        whole = (s_q.astype(F32) + f_q) * t_q.astype(F32)
        d_tail[...] += fold_line(jnp.sum(whole, axis=0, keepdims=True), spread)

    def up(k):
        return pltpu.make_async_remote_copy(
            src_ref=send_f.at[k], dst_ref=recv_f.at[k], send_sem=fs_sem.at[k], recv_sem=fr_sem.at[k],
            device_id={"ctx": after}, device_id_type=MESH,
        )

    def down(k):
        return pltpu.make_async_remote_copy(
            src_ref=send_b.at[k], dst_ref=recv_b.at[k], send_sem=bs_sem.at[k], recv_sem=br_sem.at[k],
            device_id={"ctx": before}, device_id_type=MESH,
        )

    far = (chips - 1) * SKEW
    near = jnp.minimum(pos, chips - 1 - pos)
    inner_from = jnp.where(near >= chips // 4, 2, near * SKEW + pieces)
    inner_from = jnp.minimum(inner_from, far + sub - 1)

    def slot(t, carry):
        k_f = t - pos * SKEW
        k_b = t - (chips - 1 - pos) * SKEW

        @pl.when((t < sub * steps) & (lax.rem(t, sub) == 0))
        def _():
            dense(lax.div(t, sub))

        @pl.when((k_f >= 0) & (k_f < pieces))
        def _():
            @pl.when(pos > 0)
            def _():
                up(k_f).wait_recv()

            by = scale[k_f][0:1, :]
            entering = by * unpack(recv_f[k_f])
            s_in[k_f] = entering.astype(BF16)

            @pl.when(pos < chips - 1)
            def _():
                send_f[k_f] = pack(by * (entering + fresh[k_f]))
                up(k_f).start()

        @pl.when((k_b >= 0) & (k_b < pieces))
        def _():
            @pl.when(pos < chips - 1)
            def _():
                down(k_b).wait_recv()

            by = scale[k_b][0:1, :]
            entering = by * unpack(recv_b[k_b])
            t_in[k_b] = entering.astype(BF16)

            @pl.when(pos > 0)
            def _():
                send_b[k_b] = pack(by * (entering + back[k_b]))
                down(k_b).start()

        k_i = t - inner_from

        @pl.when((k_i >= 0) & (k_i < sub * steps) & (lax.rem(k_i, sub) == 0))
        def _():
            inner(lax.div(k_i, sub))

        @pl.when(k_i == sub * steps)
        def _():
            cross()

        k_o = t - far - sub

        @pl.when((k_o >= 0) & (lax.rem(k_o, sub) == 0))
        def _():
            outer(lax.div(k_o, sub))

        return carry

    lax.fori_loop(0, far + sub + pieces, slot, 0)

    z, dt, rate = step_sizes()
    d_a = d_tail[0:1, :] + mm_exact((i_at <= j_at).astype(F32), row[...] - col[...])
    d_dt = col[...] / dt + rate * d_a
    d_raw = d_dt * jax.nn.sigmoid(z)
    sum_s[...] = jnp.zeros_like(sum_s)
    sum_s[0:1, :] = rate * jnp.sum(d_a * dt, axis=0, keepdims=True)
    sum_s[1:2, :] = jnp.sum(d_raw, axis=0, keepdims=True)
    sum_s[2:3, :] = d_skip[0:1, :]
    draw_s[...] = d_raw

    def sum_copy(j, place):
        return pltpu.make_async_remote_copy(
            src_ref=sum_s, dst_ref=sum_r.at[place], send_sem=ss_sem.at[j], recv_sem=sr_sem.at[place],
            device_id={"ctx": chips * core + j}, device_id_type=MESH,
        )

    def sum_send(j, carry):
        @pl.when(chips * core + j != me)
        def _():
            sum_copy(j, pos).start()

        return carry

    lax.fori_loop(0, chips, sum_send, 0)

    backs = [
        (dbs.at[their_rows], gb.at[:, mine_b]),
        (dcs.at[their_rows], gc.at[:, mine_b]),
        (draw_s.at[their_rows], draw_r),
    ]
    copies = []
    for at, (src, dst) in enumerate(backs):
        copy = pltpu.make_async_remote_copy(
            src_ref=src, dst_ref=dst, send_sem=out_send.at[at], recv_sem=out_recv.at[at],
            device_id={"ctx": partner}, device_id_type=MESH,
        )
        copy.start()
        copies.append(copy)
    gb[:, mine_b] = dbs[mine_rows, :]
    gc[:, mine_b] = dcs[mine_rows, :]

    @pl.when(my_half == core)
    def _():
        sum_r[pos] = sum_s[...]

    def sum_wait(j, carry):
        @pl.when(2 * j + my_half != me)
        def _():
            sum_copy(j, j).wait_recv()

        return carry

    lax.fori_loop(0, chips, sum_wait, 0)
    total = jnp.sum(sum_r[...], axis=0)
    all_s[...] = total

    def all_copy(d, place):
        return pltpu.make_async_remote_copy(
            src_ref=all_s, dst_ref=all_r.at[place], send_sem=as_sem.at[d], recv_sem=ar_sem.at[place],
            device_id={"dp": lax.rem(me_dp + d, copies_dp)}, device_id_type=MESH,
        )

    def all_send(d, carry):
        all_copy(d, d).start()
        return carry

    def all_wait(d, carry):
        all_copy(d, d).wait()
        return carry

    lax.fori_loop(1, copies_dp, all_send, 0)

    def drain(k, carry):
        @pl.when(pos < chips - 1)
        def _():
            up(k).wait_send()

        @pl.when(pos > 0)
        def _():
            down(k).wait_send()

        return carry

    lax.fori_loop(0, pieces, drain, 0)

    def drain_small(j, carry):
        @pl.when(2 * j + my_half != me)
        def _():
            par_copy(j, my_place).wait_send()

        @pl.when(chips * core + j != me)
        def _():
            sum_copy(j, pos).wait_send()

        return carry

    lax.fori_loop(0, chips, drain_small, 0)
    for copy in copies:
        copy.wait()
    gs[...] = (draw_s[mine_rows, :] + draw_r[...]).astype(BF16)
    lax.fori_loop(1, copies_dp, all_wait, 0)
    all_r[0] = total
    heads = total.shape[1]
    head = lax.broadcasted_iota(jnp.int32, (heads, heads), 0)
    lane = lax.broadcasted_iota(jnp.int32, (heads, heads), 1)
    pick = ((head == me * held + lane) & (lane < held)).astype(F32)
    gp[...] = mm_exact(jnp.sum(all_r[...], axis=0), pick)


def finish(gb, gc, gs, gp, gb_out, gc_out, gs_out, decay_out, bias_out, skip_out):
    gb_out[...] = gb[...]
    gc_out[...] = gc[...]
    gs_out[...] = gs[...]
    span = decay_out.shape[1]
    decay_out[...] = gp[0:1, :span]
    bias_out[...] = gp[1:2, :span]
    skip_out[...] = gp[2:3, :span]


def run(x, g, b, c, raw, bias, log_rate, chips, copies_dp):
    tok, wide = x.shape
    half = wide // 2
    cols = b.shape[1] // 2
    groups = cols // STATE
    rows = 2 * tok
    pieces = half // LANES
    heads = raw.shape[1]
    steps = half // WIDE
    anywhere = pl.BlockSpec(memory_space=pl.ANY)
    inside = pl.BlockSpec(memory_space=pltpu.VMEM)
    scalars = pl.BlockSpec(memory_space=pltpu.SMEM)
    state16 = pltpu.VMEM((pieces, STATE, LANES), BF16)
    state32 = pltpu.VMEM((pieces, STATE, LANES), F32)
    wide16 = pltpu.VMEM((rows, half), BF16)
    tile = pltpu.VMEM((8, heads), F32)
    dma = pltpu.SemaphoreType.DMA
    moves = 3 + 2 * steps
    parts = pl.pallas_call(
        partial(kernel, chips, copies_dp),
        out_shape=(
            jax.ShapeDtypeStruct((tok, 2 * cols), F32),
            jax.ShapeDtypeStruct((tok, 2 * cols), F32),
            jax.ShapeDtypeStruct((tok, heads), BF16),
            jax.ShapeDtypeStruct((8, heads), F32),
        ),
        in_specs=[anywhere] * 5 + [scalars] * 2,
        out_specs=(inside,) * 4,
        scratch_shapes=[
            wide16, wide16,
            pltpu.VMEM((rows, cols), BF16), pltpu.VMEM((rows, cols), BF16),
            pltpu.VMEM((rows, heads), BF16),
            pltpu.VMEM((rows, 2 * LANES), BF16), pltpu.VMEM((rows, 2 * LANES), BF16),
            wide16, wide16, wide16, wide16,
            state32, state32, state16, state16, state16, state16, state16, state16,
            pltpu.VMEM((pieces, 8, LANES), F32),
            pltpu.VMEM((groups, rows, rows), F32),
            pltpu.VMEM((groups, rows, rows), BF16), pltpu.VMEM((groups, rows, rows), BF16),
            pltpu.VMEM((groups, STATE, rows), BF16), pltpu.VMEM((groups, STATE, rows), BF16),
            pltpu.VMEM((rows, LANES), F32), pltpu.VMEM((rows, LANES), F32),
            pltpu.VMEM((rows, cols), F32), pltpu.VMEM((rows, cols), F32),
            tile, tile,
            pltpu.VMEM((rows, heads), F32), pltpu.VMEM((tok, heads), F32),
            tile, pltpu.VMEM((chips, 8, heads), F32),
            tile, pltpu.VMEM((chips, 8, heads), F32),
            tile, pltpu.VMEM((copies_dp, 8, heads), F32),
            dma((moves,)), dma((moves,)), dma((moves,)),
            dma((pieces,)), dma((pieces,)), dma((pieces,)), dma((pieces,)),
            dma((3,)), dma((3,)),
            dma((chips,)), dma((chips,)), dma((chips,)), dma((chips,)),
            dma((copies_dp,)), dma((copies_dp,)),
        ],
        compiler_params=pltpu.CompilerParams(
            collective_id=0, has_side_effects=True, vmem_limit_bytes=60 * 1024 * 1024
        ),
        name="scan_backward",
    )(x, g, b, c, raw, bias, log_rate)
    line = jax.ShapeDtypeStruct((1, bias.shape[0]), F32)
    return pl.pallas_call(
        finish,
        out_shape=tuple(jax.ShapeDtypeStruct(v.shape, v.dtype) for v in parts[:3]) + (line,) * 3,
        in_specs=[inside] * 4,
        out_specs=(inside,) * 6,
        compiler_params=pltpu.CompilerParams(vmem_limit_bytes=60 * 1024 * 1024),
        name="results",
    )(*parts)


def local(x_tokens, grad_out, step_raw, step_bias, decay_log, b_proj, c_proj):
    gb, gc, gs, decay, bias, skip = run(
        x_tokens[0], grad_out[0], b_proj[0], c_proj[0], step_raw[0], step_bias, decay_log,
        lax.axis_size("ctx") // 2, lax.axis_size("dp"),
    )
    return (gb[None], gc[None], gs[None], decay[0], bias[0], skip[0])


def solution(mesh):
    tokens = P("dp", "ctx", None)
    return jax.shard_map(
        local,
        mesh=mesh,
        in_specs=(tokens, tokens, tokens, P("ctx"), P("ctx"), tokens, tokens),
        out_specs=(tokens, tokens, tokens, P("ctx"), P("ctx"), P("ctx")),
        check_vma=False,
    )
```

```python
from functools import partial

import jax
import jax.numpy as jnp
from jax import lax
from jax.experimental import pallas as pl
from jax.experimental.pallas import tpu as pltpu
from jax.sharding import PartitionSpec as P

HEADDIM = 64
STATE = 128
LANES = 128
WIDE = 512
SKEW = 5
DELAY = 12
F32 = jnp.float32
BF16 = jnp.bfloat16
MESH = pl.DeviceIdType.MESH


def mm(a, b):
    return lax.dot_general(a, b, (((1,), (0,)), ((), ())), preferred_element_type=F32)


def mm_nt(a, b):
    return lax.dot_general(a, b, (((1,), (1,)), ((), ())), preferred_element_type=F32)


def halves(v):
    high = v.astype(BF16)
    return high, (v - high.astype(F32)).astype(BF16)


def thirds(v):
    high = v.astype(BF16)
    rest = v - high.astype(F32)
    middle = rest.astype(BF16)
    return high, middle, (rest - middle.astype(F32)).astype(BF16)


def pack(v):
    return (v * jnp.abs(v)).astype(BF16)


def unpack(code):
    u = code.astype(F32)
    root = jnp.sqrt(jnp.abs(u))
    return jnp.where(u < 0.0, -root, root)


def kernel(
    chips, copies_dp, x, g, b, c, raw, bias, log_rate,
    gb, gc, gs, gp,
    xs, gr, bs, cs, rs,
    eh, fh, eg, fx, eg_low, fx_low, fresh, back, send_f, send_b, recv_f, recv_b, recv_e, kept, scale,
    decay, past_s, past_r,
    gram, mix, mixt, bt, ct, row, col, dcs, dbs, d_skip, d_tail, draw_s, draw_r, gs_v,
    par, par_r, sum_s, sum_r, all_s, all_r,
    own_sem, pair_send, pair_recv, fs_sem, fr_sem, bs_sem, br_sem, er_sem, ea_sem, eb_sem,
    past_sem, out_send, out_recv,
    ps_sem, pr_sem, ss_sem, sr_sem, as_sem, ar_sem,
):
    me = lax.axis_index("ctx")
    me_dp = lax.axis_index("dp")
    core = lax.rem(me, 2)
    pos = lax.div(me, 2)
    count = 2 * chips
    partner = me + 1 - 2 * core
    run_len = chips // 2
    side = lax.div(pos, run_len)
    loc = lax.rem(pos, run_len)
    depth = jnp.where(side == 1, loc, run_len - 1 - loc)

    def chip_at(run, at):
        return (run * run_len + at) * 2 + core

    def at_depth(d):
        return chip_at(side, jnp.where(side == 1, d, run_len - 1 - d))

    tok = x.shape[0]
    rows = 2 * tok
    half = xs.shape[1]
    cols = bs.shape[1]
    groups = cols // STATE
    steps = half // WIDE
    per_group = steps // groups
    heads_w = WIDE // HEADDIM
    pieces = half // LANES
    sub = WIDE // LANES
    first_head = core * (half // HEADDIM)
    my_half = lax.div(me, chips)
    my_place = lax.rem(me, chips)

    mine_rows = pl.ds(pl.multiple_of(core * tok, tok), tok)
    their_rows = pl.ds(pl.multiple_of((1 - core) * tok, tok), tok)
    mine_b = pl.ds(pl.multiple_of(core * cols, cols), cols)
    their_b = pl.ds(pl.multiple_of((1 - core) * cols, cols), cols)

    def lanes_of(q):
        return pl.ds(pl.multiple_of(q * WIDE, WIDE), WIDE)

    def moves_of(q):
        mine = pl.ds(pl.multiple_of(core * half + q * WIDE, WIDE), WIDE)
        theirs = pl.ds(pl.multiple_of((1 - core) * half + q * WIDE, WIDE), WIDE)
        return [
            (x.at[:, mine], x.at[:, theirs], xs.at[mine_rows, lanes_of(q)], 3 + 2 * q),
            (g.at[:, mine], g.at[:, theirs], gr.at[mine_rows, lanes_of(q)], 4 + 2 * q),
        ]

    small_moves = [
        (raw, raw, rs.at[mine_rows], 0),
        (b.at[:, mine_b], b.at[:, their_b], bs.at[mine_rows], 1),
        (c.at[:, mine_b], c.at[:, their_b], cs.at[mine_rows], 2),
    ]

    def own_copy(move):
        return pltpu.make_async_copy(move[0], move[2], own_sem.at[move[3]])

    def pair_copy(move):
        return pltpu.make_async_remote_copy(
            src_ref=move[1], dst_ref=move[2],
            send_sem=pair_send.at[move[3]], recv_sem=pair_recv.at[move[3]],
            device_id={"ctx": partner}, device_id_type=MESH,
        )

    held = bias.shape[0]
    lane = lax.broadcasted_iota(jnp.int32, (8, par.shape[1]), 1)
    line = lax.broadcasted_iota(jnp.int32, (8, par.shape[1]), 0)
    tile = jnp.zeros(par.shape, F32)
    for k in range(held):
        here = lane == me * held + k
        tile = jnp.where(here & (line == 0), bias[k], tile)
        tile = jnp.where(here & (line == 1), log_rate[k], tile)
    par[...] = tile

    for move in small_moves:
        own_copy(move).start()

    def start_own(q, carry):
        for move in moves_of(q):
            own_copy(move).start()
        return carry

    lax.fori_loop(0, steps, start_own, 0)

    barrier = pltpu.get_barrier_semaphore()

    def greet(d, carry):
        pl.semaphore_signal(
            barrier, inc=1, device_id={"ctx": lax.rem(me + d, count)}, device_id_type=MESH
        )
        return carry

    def greet_dp(d, carry):
        pl.semaphore_signal(
            barrier, inc=1, device_id={"dp": lax.rem(me_dp + d, copies_dp)}, device_id_type=MESH
        )
        return carry

    lax.fori_loop(1, count, greet, 0)
    lax.fori_loop(1, copies_dp, greet_dp, 0)
    pl.semaphore_wait(barrier, count - 1 + copies_dp - 1)

    def par_copy(j, place):
        return pltpu.make_async_remote_copy(
            src_ref=par, dst_ref=par_r.at[place], send_sem=ps_sem.at[j], recv_sem=pr_sem.at[place],
            device_id={"ctx": 2 * j + my_half}, device_id_type=MESH,
        )

    def par_send(j, carry):
        @pl.when(2 * j + my_half != me)
        def _():
            par_copy(j, my_place).start()

        return carry

    lax.fori_loop(0, chips, par_send, 0)

    for move in small_moves:
        pair_copy(move).start()

    def start_pair(q, carry):
        for move in moves_of(q):
            pair_copy(move).start()
        return carry

    lax.fori_loop(0, steps, start_pair, 0)

    gram[...] = jnp.zeros_like(gram)
    row[...] = jnp.zeros_like(row)
    col[...] = jnp.zeros_like(col)
    dcs[...] = jnp.zeros_like(dcs)
    dbs[...] = jnp.zeros_like(dbs)
    d_skip[...] = jnp.zeros_like(d_skip)
    d_tail[...] = jnp.zeros_like(d_tail)

    @pl.when(loc == 0)
    def _():
        recv_f[...] = jnp.zeros_like(recv_f)

    @pl.when(loc == run_len - 1)
    def _():
        recv_b[...] = jnp.zeros_like(recv_b)

    @pl.when(depth == 0)
    def _():
        past_r[...] = jnp.ones_like(past_r)

    for move in small_moves:
        own_copy(move).wait()
        pair_copy(move).wait()

    i_at = lax.broadcasted_iota(jnp.int32, (rows, rows), 0)
    j_at = lax.broadcasted_iota(jnp.int32, (rows, rows), 1)
    causal = i_at >= j_at
    for at in range(groups):
        span = slice(at * STATE, (at + 1) * STATE)
        b_at = bs[:, span]
        c_at = cs[:, span]
        bt[at] = b_at.astype(F32).T.astype(BF16)
        ct[at] = c_at.astype(F32).T.astype(BF16)
        scores = jnp.where(causal, mm_nt(c_at, b_at), 0.0)
        mix[at] = scores.astype(BF16)
        mixt[at] = scores.T.astype(BF16)

    @pl.when(my_half == core)
    def _():
        par_r[my_place] = par[...]

    def par_wait(j, carry):
        @pl.when(chips * core + j != me)
        def _():
            par_copy(j, j).wait_recv()

        return carry

    lax.fori_loop(0, chips, par_wait, 0)

    def step_sizes():
        params = jnp.sum(par_r[...], axis=0)
        z = rs[...].astype(F32) + params[0:1, :]
        dt = jnp.maximum(z, 0.0) + jnp.log1p(jnp.exp(-jnp.abs(z)))
        lane = lax.broadcasted_iota(jnp.int32, (1, z.shape[1]), 1)
        own = lax.div(lane, z.shape[1] // 2) == core
        return z, dt, jnp.where(own, -jnp.exp(params[1:2, :]), 0.0)

    z, dt, rate = step_sizes()
    ones = causal.astype(F32).astype(BF16)
    cum = sum(mm(ones, part) for part in thirds(dt * rate))
    mid = cum[rows - 1 : rows, :] * 0.5
    e_hi, e_lo = halves(jnp.exp(cum - mid))
    f_hi, f_lo = halves(jnp.exp(mid - cum) * dt)
    eh[:, :LANES] = e_hi
    eh[:, LANES:] = e_lo
    fh[:, :LANES] = f_hi
    fh[:, LANES:] = f_lo
    decay[...] = jnp.broadcast_to(jnp.exp(2.0 * mid), decay.shape)
    a_hi, a_lo = halves(jnp.broadcast_to(jnp.exp(mid), (16, LANES)))
    a_both = jnp.concatenate([a_hi, a_lo], axis=1)

    def spread_of(q):
        head = lax.broadcasted_iota(jnp.int32, (LANES, WIDE), 0)
        lane = lax.broadcasted_iota(jnp.int32, (LANES, WIDE), 1)
        return (head == first_head + q * heads_w + lax.div(lane, HEADDIM)).astype(F32).astype(BF16)

    def fold(v, spread):
        high, low = halves(v)
        return mm_nt(high, spread) + mm_nt(low, spread)

    def fold_line(v, spread):
        return fold(jnp.broadcast_to(v, (16, WIDE)), spread)[0:8, :]

    def full(high, low, here):
        return high[:, here].astype(F32) + low[:, here].astype(F32)

    def dense(q):
        for move in moves_of(q):
            own_copy(move).wait()
            pair_copy(move).wait()
        at = lax.div(q, per_group)
        here = lanes_of(q)
        spread = spread_of(q)
        both = jnp.concatenate([spread, spread], axis=0)
        x_q = xs[:, here].astype(F32)
        g_q = gr[:, here].astype(F32)
        d_skip[...] += fold_line(jnp.sum(x_q * g_q, axis=0, keepdims=True), spread)
        eg_q, eg_rest = halves(mm(eh[...], both) * g_q)
        fx_q, fx_rest = halves(mm(fh[...], both) * x_q)
        eg[:, here] = eg_q
        fx[:, here] = fx_q
        eg_low[:, here] = eg_rest
        fx_low[:, here] = fx_rest
        fresh_q = mm(bt[at], fx_q) + mm(bt[at], fx_rest)
        back_q = mm(ct[at], eg_q) + mm(ct[at], eg_rest)
        scale_q = mm(a_both, both)
        for k in range(sub):
            span = slice(k * LANES, (k + 1) * LANES)
            fresh[q * sub + k] = fresh_q[:, span]
            back[q * sub + k] = back_q[:, span]
            scale[q * sub + k] = scale_q[0:8, span]

    def inner(q):
        at = lax.div(q, per_group)
        here = lanes_of(q)
        spread = spread_of(q)
        eg_q = eg[:, here]
        fx_q = fx[:, here]
        gram[at] += mm_nt(eg_q, fx_q)
        y_q = mm(mix[at], fx_q) + mm(mix[at], fx_low[:, here])
        v_q = mm(mixt[at], eg_q) + mm(mixt[at], eg_low[:, here])
        row[...] += fold(full(eg, eg_low, here) * y_q, spread)
        col[...] += fold(full(fx, fx_low, here) * v_q, spread)

    def cross():
        for at in range(groups):
            span = slice(at * STATE, (at + 1) * STATE)
            cot = jnp.where(causal, gram[at], 0.0)
            dcs[:, span] += mm(cot.astype(BF16), bs[:, span])
            dbs[:, span] += mm(cot.T.astype(BF16), cs[:, span])

    def wide(ref, q):
        return jnp.concatenate([ref[q * sub + k] for k in range(sub)], axis=1)

    def state_part(q, v, spread):
        here = lanes_of(q)
        span = pl.ds(pl.multiple_of(lax.div(q, per_group) * STATE, STATE), STATE)
        row[...] += fold(full(eg, eg_low, here) * mm(cs[:, span], v), spread)
        dcs[:, span] += mm_nt(eg[:, here], v)

    def cotangent_part(q, v, spread):
        here = lanes_of(q)
        span = pl.ds(pl.multiple_of(lax.div(q, per_group) * STATE, STATE), STATE)
        col[...] += fold(full(fx, fx_low, here) * mm(bs[:, span], v), spread)
        dbs[:, span] += mm_nt(fx[:, here], v)

    def outer_near(q):
        by = wide(scale, q)[0:1, :]
        spread = spread_of(q)

        @pl.when(side == 0)
        def _():
            v = (by * unpack(wide(recv_f, q))).astype(BF16)
            kept[q] = v
            state_part(q, v, spread)

        @pl.when(side == 1)
        def _():
            v = (by * unpack(wide(recv_b, q))).astype(BF16)
            kept[q] = v
            cotangent_part(q, v, spread)

    def outer_far(q):
        by = wide(scale, q)[0:1, :]
        spread = spread_of(q)
        both = jnp.concatenate([spread, spread], axis=0)
        past = jnp.concatenate(halves(jnp.broadcast_to(past_r[0:1, :], (16, LANES))), axis=1)
        handed = mm(past, both)[0:1, :] * unpack(wide(recv_e, q))
        f_q = wide(fresh, q)

        def tail(s_q, t_q):
            whole = (s_q.astype(F32) + f_q) * t_q.astype(F32)
            d_tail[...] += fold_line(jnp.sum(whole, axis=0, keepdims=True), spread)

        @pl.when(side == 1)
        def _():
            v = (by * (unpack(wide(recv_f, q)) + handed)).astype(BF16)
            tail(v, kept[q])
            state_part(q, v, spread)

        @pl.when(side == 0)
        def _():
            v = (by * (unpack(wide(recv_b, q)) + handed)).astype(BF16)
            tail(kept[q], v)
            cotangent_part(q, v, spread)

    def copy_to(src, dst, send_sem, recv_sem, other):
        return pltpu.make_async_remote_copy(
            src_ref=src, dst_ref=dst, send_sem=send_sem, recv_sem=recv_sem,
            device_id={"ctx": other}, device_id_type=MESH,
        )

    def up(k):
        return copy_to(send_f.at[k], recv_f.at[k], fs_sem.at[k], fr_sem.at[k], chip_at(side, loc + 1))

    def down(k):
        return copy_to(send_b.at[k], recv_b.at[k], bs_sem.at[k], br_sem.at[k], chip_at(side, loc - 1))

    def over_f(k):
        return copy_to(send_f.at[k], recv_e.at[k], fs_sem.at[k], er_sem.at[k], chip_at(1 - side, loc))

    def over_b(k):
        return copy_to(send_b.at[k], recv_e.at[k], bs_sem.at[k], er_sem.at[k], chip_at(1 - side, loc))

    mid_len = run_len // 2
    last = depth == run_len - 1
    next_a = jnp.where(last, 0, jnp.where(depth < mid_len, depth + 1, depth - 1))
    has_a = ((depth < mid_len - 1) | ((depth > mid_len) & (depth < run_len - 1))) | (
        last & (run_len >= 2)
    )
    has_b = last & (run_len - 2 >= mid_len)

    def on_a(k):
        return copy_to(recv_e.at[k], recv_e.at[k], ea_sem.at[k], er_sem.at[k], at_depth(next_a))

    def on_b(k):
        return copy_to(
            recv_e.at[k], recv_e.at[k], eb_sem.at[k], er_sem.at[k], at_depth(run_len - 2)
        )

    def past_on():
        return copy_to(past_s, past_r, past_sem.at[0], past_sem.at[1], at_depth(depth + 1))

    up_next = loc < run_len - 1
    up_over = (loc == run_len - 1) & (side == 0)
    down_next = loc > 0
    down_over = (loc == 0) & (side == 1)
    from_f = 1 + loc * SKEW + jnp.where(side == 1, DELAY, 0)
    from_b = 1 + (run_len - 1 - loc) * SKEW + jnp.where(side == 0, DELAY, 0)
    hops = jnp.where(last, 0, jnp.where(depth < mid_len, depth + 1, run_len - 1 - depth))
    handed_at = 3 + run_len * SKEW
    from_e = handed_at + hops * SKEW
    far = handed_at + mid_len * SKEW
    far_from = far + sub + 2
    near_from = jnp.minimum(jnp.where(side == 0, from_f, from_b) + pieces + 1, far_from)
    early = depth <= mid_len
    gap = jnp.where(early, sub, 2)
    inner_from = jnp.where(early, 2, (run_len - 1 - depth) * SKEW + pieces + 2)
    inner_from = jnp.minimum(inner_from, far + sub + pieces - steps * gap - 1)

    def slot(t, carry):
        k_f = t - from_f
        k_b = t - from_b
        k_e = t - from_e

        @pl.when((t < sub * steps) & (lax.rem(t, sub) == 0))
        def _():
            dense(lax.div(t, sub))

        @pl.when((k_f >= 0) & (k_f < pieces))
        def _():
            @pl.when(loc > 0)
            def _():
                up(k_f).wait_recv()

            @pl.when(up_next | up_over)
            def _():
                by = scale[k_f][0:1, :]
                send_f[k_f] = pack(by * (by * unpack(recv_f[k_f]) + fresh[k_f]))

            @pl.when(up_next)
            def _():
                up(k_f).start()

            @pl.when(up_over)
            def _():
                over_f(k_f).start()

        @pl.when((k_b >= 0) & (k_b < pieces))
        def _():
            @pl.when(loc < run_len - 1)
            def _():
                down(k_b).wait_recv()

            @pl.when(down_next | down_over)
            def _():
                by = scale[k_b][0:1, :]
                send_b[k_b] = pack(by * (by * unpack(recv_b[k_b]) + back[k_b]))

            @pl.when(down_next)
            def _():
                down(k_b).start()

            @pl.when(down_over)
            def _():
                over_b(k_b).start()

        @pl.when((k_e >= 0) & (k_e < pieces))
        def _():
            on_a(k_e).wait_recv()

            @pl.when(has_a)
            def _():
                on_a(k_e).start()

            @pl.when(has_b)
            def _():
                on_b(k_e).start()

        @pl.when(t == depth * SKEW + DELAY)
        def _():
            @pl.when(depth > 0)
            def _():
                past_on().wait_recv()

            @pl.when(depth < run_len - 1)
            def _():
                past_s[...] = past_r[...] * decay[...]
                past_on().start()

        k_i = t - inner_from

        @pl.when((k_i >= 0) & (k_i < steps * gap) & (lax.rem(k_i, gap) == 0))
        def _():
            inner(lax.div(k_i, gap))

        @pl.when(k_i == steps * gap)
        def _():
            cross()

        k_n = t - near_from

        @pl.when((k_n >= 0) & (k_n < steps * sub) & (lax.rem(k_n, sub) == 0))
        def _():
            outer_near(lax.div(k_n, sub))

        k_o = t - far_from

        @pl.when((k_o >= 0) & (k_o < steps * sub) & (lax.rem(k_o, sub) == 0))
        def _():
            outer_far(lax.div(k_o, sub))

        return carry

    lax.fori_loop(0, far_from + pieces, slot, 0)

    z, dt, rate = step_sizes()
    ones = (i_at <= j_at).astype(F32).astype(BF16)
    d_a = d_tail[0:1, :] + sum(mm(ones, part) for part in thirds(row[...] - col[...]))
    d_dt = col[...] / dt + rate * d_a
    d_raw = d_dt * jax.nn.sigmoid(z)
    sum_s[...] = jnp.zeros_like(sum_s)
    sum_s[0:1, :] = rate * jnp.sum(d_a * dt, axis=0, keepdims=True)
    sum_s[1:2, :] = jnp.sum(d_raw, axis=0, keepdims=True)
    sum_s[2:3, :] = d_skip[0:1, :]
    draw_s[...] = d_raw

    def sum_copy(j, place):
        return pltpu.make_async_remote_copy(
            src_ref=sum_s, dst_ref=sum_r.at[place], send_sem=ss_sem.at[j], recv_sem=sr_sem.at[place],
            device_id={"ctx": chips * core + j}, device_id_type=MESH,
        )

    def sum_send(j, carry):
        @pl.when(chips * core + j != me)
        def _():
            sum_copy(j, pos).start()

        return carry

    lax.fori_loop(0, chips, sum_send, 0)

    backs = [
        (dbs.at[their_rows], gb.at[:, mine_b]),
        (dcs.at[their_rows], gc.at[:, mine_b]),
        (draw_s.at[their_rows], draw_r),
    ]
    copies = []
    for at, (src, dst) in enumerate(backs):
        copy = pltpu.make_async_remote_copy(
            src_ref=src, dst_ref=dst, send_sem=out_send.at[at], recv_sem=out_recv.at[at],
            device_id={"ctx": partner}, device_id_type=MESH,
        )
        copy.start()
        copies.append(copy)
    own_b = pltpu.make_async_copy(dbs.at[mine_rows], gb.at[:, mine_b], own_sem.at[0])
    own_c = pltpu.make_async_copy(dcs.at[mine_rows], gc.at[:, mine_b], own_sem.at[1])
    own_b.start()
    own_c.start()

    @pl.when(my_half == core)
    def _():
        sum_r[pos] = sum_s[...]

    def sum_wait(j, carry):
        @pl.when(2 * j + my_half != me)
        def _():
            sum_copy(j, j).wait_recv()

        return carry

    lax.fori_loop(0, chips, sum_wait, 0)
    total = jnp.sum(sum_r[...], axis=0)
    all_s[...] = total

    def all_copy(d, place):
        return pltpu.make_async_remote_copy(
            src_ref=all_s, dst_ref=all_r.at[place], send_sem=as_sem.at[d], recv_sem=ar_sem.at[place],
            device_id={"dp": lax.rem(me_dp + d, copies_dp)}, device_id_type=MESH,
        )

    def all_send(d, carry):
        all_copy(d, d).start()
        return carry

    def all_wait(d, carry):
        all_copy(d, d).wait()
        return carry

    lax.fori_loop(1, copies_dp, all_send, 0)

    def drain(k, carry):
        @pl.when(up_next | up_over)
        def _():
            up(k).wait_send()

        @pl.when(down_next | down_over)
        def _():
            down(k).wait_send()

        @pl.when(has_a)
        def _():
            on_a(k).wait_send()

        @pl.when(has_b)
        def _():
            on_b(k).wait_send()

        return carry

    lax.fori_loop(0, pieces, drain, 0)

    def drain_small(j, carry):
        @pl.when(2 * j + my_half != me)
        def _():
            par_copy(j, my_place).wait_send()

        @pl.when(chips * core + j != me)
        def _():
            sum_copy(j, pos).wait_send()

        return carry

    lax.fori_loop(0, chips, drain_small, 0)

    @pl.when(depth < run_len - 1)
    def _():
        past_on().wait_send()

    for copy in copies:
        copy.wait()
    gs_v[...] = (draw_s[mine_rows, :] + draw_r[...]).astype(BF16)
    own_s = pltpu.make_async_copy(gs_v, gs, own_sem.at[2])
    own_s.start()
    lax.fori_loop(1, copies_dp, all_wait, 0)
    all_r[0] = total
    own_b.wait()
    own_c.wait()
    own_s.wait()
    heads = total.shape[1]
    head = lax.broadcasted_iota(jnp.int32, (heads, heads), 0)
    lane = lax.broadcasted_iota(jnp.int32, (heads, heads), 1)
    pick = ((head == me * held + lane) & (lane < held)).astype(F32).astype(BF16)
    gp[...] = sum(mm(part, pick) for part in thirds(jnp.sum(all_r[...], axis=0)))


def finish(gb, gc, gs, gp, gb_out, gc_out, gs_out, decay_out, bias_out, skip_out):
    gb_out[...] = gb[...]
    gc_out[...] = gc[...]
    gs_out[...] = gs[...]
    span = decay_out.shape[1]
    decay_out[...] = gp[0:1, :span]
    bias_out[...] = gp[1:2, :span]
    skip_out[...] = gp[2:3, :span]


def run(x, g, b, c, raw, bias, log_rate, chips, copies_dp):
    tok, wide = x.shape
    half = wide // 2
    cols = b.shape[1] // 2
    groups = cols // STATE
    rows = 2 * tok
    pieces = half // LANES
    heads = raw.shape[1]
    steps = half // WIDE
    anywhere = pl.BlockSpec(memory_space=pl.ANY)
    inside = pl.BlockSpec(memory_space=pltpu.VMEM)
    scalars = pl.BlockSpec(memory_space=pltpu.SMEM)
    state16 = pltpu.VMEM((pieces, STATE, LANES), BF16)
    state32 = pltpu.VMEM((pieces, STATE, LANES), F32)
    wide16 = pltpu.VMEM((rows, half), BF16)
    tile = pltpu.VMEM((8, heads), F32)
    dma = pltpu.SemaphoreType.DMA
    moves = 3 + 2 * steps
    parts = pl.pallas_call(
        partial(kernel, chips, copies_dp),
        out_shape=(
            jax.ShapeDtypeStruct((tok, 2 * cols), F32),
            jax.ShapeDtypeStruct((tok, 2 * cols), F32),
            jax.ShapeDtypeStruct((tok, heads), BF16),
            jax.ShapeDtypeStruct((8, heads), F32),
        ),
        in_specs=[anywhere] * 5 + [scalars] * 2,
        out_specs=(anywhere,) * 3 + (inside,),
        scratch_shapes=[
            wide16, wide16,
            pltpu.VMEM((rows, cols), BF16), pltpu.VMEM((rows, cols), BF16),
            pltpu.VMEM((rows, heads), BF16),
            pltpu.VMEM((rows, 2 * LANES), BF16), pltpu.VMEM((rows, 2 * LANES), BF16),
            wide16, wide16, wide16, wide16,
            state32, state32, state16, state16, state16, state16, state16,
            pltpu.VMEM((steps, STATE, WIDE), BF16),
            pltpu.VMEM((pieces, 8, LANES), F32),
            tile, tile, tile,
            pltpu.VMEM((groups, rows, rows), F32),
            pltpu.VMEM((groups, rows, rows), BF16), pltpu.VMEM((groups, rows, rows), BF16),
            pltpu.VMEM((groups, STATE, rows), BF16), pltpu.VMEM((groups, STATE, rows), BF16),
            pltpu.VMEM((rows, LANES), F32), pltpu.VMEM((rows, LANES), F32),
            pltpu.VMEM((rows, cols), F32), pltpu.VMEM((rows, cols), F32),
            tile, tile,
            pltpu.VMEM((rows, heads), F32), pltpu.VMEM((tok, heads), F32),
            pltpu.VMEM((tok, heads), BF16),
            tile, pltpu.VMEM((chips, 8, heads), F32),
            tile, pltpu.VMEM((chips, 8, heads), F32),
            tile, pltpu.VMEM((copies_dp, 8, heads), F32),
            dma((moves,)), dma((moves,)), dma((moves,)),
            dma((pieces,)), dma((pieces,)), dma((pieces,)), dma((pieces,)),
            dma((pieces,)), dma((pieces,)), dma((pieces,)),
            dma((2,)),
            dma((3,)), dma((3,)),
            dma((chips,)), dma((chips,)), dma((chips,)), dma((chips,)),
            dma((copies_dp,)), dma((copies_dp,)),
        ],
        compiler_params=pltpu.CompilerParams(
            collective_id=0, has_side_effects=True, vmem_limit_bytes=60 * 1024 * 1024
        ),
        name="scan_backward",
    )(x, g, b, c, raw, bias, log_rate)
    line = jax.ShapeDtypeStruct((1, bias.shape[0]), F32)
    return pl.pallas_call(
        finish,
        out_shape=tuple(jax.ShapeDtypeStruct(v.shape, v.dtype) for v in parts[:3]) + (line,) * 3,
        in_specs=[inside] * 4,
        out_specs=(inside,) * 6,
        compiler_params=pltpu.CompilerParams(vmem_limit_bytes=60 * 1024 * 1024),
        name="results",
    )(*parts)


def local(x_tokens, grad_out, step_raw, step_bias, decay_log, b_proj, c_proj):
    gb, gc, gs, decay, bias, skip = run(
        x_tokens[0], grad_out[0], b_proj[0], c_proj[0], step_raw[0], step_bias, decay_log,
        lax.axis_size("ctx") // 2, lax.axis_size("dp"),
    )
    return (gb[None], gc[None], gs[None], decay[0], bias[0], skip[0])


def solution(mesh):
    tokens = P("dp", "ctx", None)
    return jax.shard_map(
        local,
        mesh=mesh,
        in_specs=(tokens, tokens, tokens, P("ctx"), P("ctx"), tokens, tokens),
        out_specs=(tokens, tokens, tokens, P("ctx"), P("ctx"), P("ctx")),
        check_vma=False,
    )
```

```python
from functools import partial

import jax
import jax.numpy as jnp
from jax import lax
from jax.experimental import pallas as pl
from jax.experimental.pallas import tpu as pltpu
from jax.sharding import PartitionSpec as P

HEADDIM = 64
STATE = 128
LANES = 128
WIDE = 512
SKEW = 5
DELAY = 12
F32 = jnp.float32
BF16 = jnp.bfloat16
MESH = pl.DeviceIdType.MESH


def mm(a, b):
    return lax.dot_general(a, b, (((1,), (0,)), ((), ())), preferred_element_type=F32)


def mm_nt(a, b):
    return lax.dot_general(a, b, (((1,), (1,)), ((), ())), preferred_element_type=F32)


def halves(v):
    high = v.astype(BF16)
    return high, (v - high.astype(F32)).astype(BF16)


def thirds(v):
    high = v.astype(BF16)
    rest = v - high.astype(F32)
    middle = rest.astype(BF16)
    return high, middle, (rest - middle.astype(F32)).astype(BF16)


def pack(v):
    return (v * jnp.abs(v)).astype(BF16)


def unpack(code):
    u = code.astype(F32)
    root = jnp.sqrt(jnp.abs(u))
    return jnp.where(u < 0.0, -root, root)


def kernel(
    chips, copies_dp, x, g, b, c, raw, bias, log_rate,
    gb, gc, gs, gp,
    xs, gr, bs, cs, rs,
    eh, fh, eg, fx, eg_low, fx_low, fresh, back, send_f, send_b, recv_f, recv_b, recv_e, kept, scale,
    decay, past_s, past_r,
    gram, mix, mixt, bt, ct, row, col, dcs, dbs, d_skip, d_tail, draw_s, draw_r, gs_v,
    par, par_r, sum_s, sum_r, all_s, all_r,
    own_sem, pair_send, pair_recv, fs_sem, fr_sem, bs_sem, br_sem, er_sem, ea_sem, eb_sem,
    past_sem, out_send, out_recv,
    ps_sem, pr_sem, ss_sem, sr_sem, as_sem, ar_sem,
):
    me = lax.axis_index("ctx")
    me_dp = lax.axis_index("dp")
    core = lax.rem(me, 2)
    pos = lax.div(me, 2)
    count = 2 * chips
    partner = me + 1 - 2 * core
    run_len = chips // 2
    side = lax.div(pos, run_len)
    loc = lax.rem(pos, run_len)
    depth = jnp.where(side == 1, loc, run_len - 1 - loc)

    def chip_at(run, at):
        return (run * run_len + at) * 2 + core

    def at_depth(d):
        return chip_at(side, jnp.where(side == 1, d, run_len - 1 - d))

    tok = x.shape[0]
    rows = 2 * tok
    half = xs.shape[1]
    cols = bs.shape[1]
    groups = cols // STATE
    steps = half // WIDE
    per_group = steps // groups
    heads_w = WIDE // HEADDIM
    pieces = half // LANES
    sub = WIDE // LANES
    first_head = core * (half // HEADDIM)
    my_half = lax.div(me, chips)
    my_place = lax.rem(me, chips)

    mine_rows = pl.ds(pl.multiple_of(core * tok, tok), tok)
    their_rows = pl.ds(pl.multiple_of((1 - core) * tok, tok), tok)
    mine_b = pl.ds(pl.multiple_of(core * cols, cols), cols)
    their_b = pl.ds(pl.multiple_of((1 - core) * cols, cols), cols)

    def lanes_of(q):
        return pl.ds(pl.multiple_of(q * WIDE, WIDE), WIDE)

    def moves_of(q):
        mine = pl.ds(pl.multiple_of(core * half + q * WIDE, WIDE), WIDE)
        theirs = pl.ds(pl.multiple_of((1 - core) * half + q * WIDE, WIDE), WIDE)
        return [
            (x.at[:, mine], x.at[:, theirs], xs.at[mine_rows, lanes_of(q)], 3 + 2 * q),
            (g.at[:, mine], g.at[:, theirs], gr.at[mine_rows, lanes_of(q)], 4 + 2 * q),
        ]

    small_moves = [
        (raw, raw, rs.at[mine_rows], 0),
        (b.at[:, mine_b], b.at[:, their_b], bs.at[mine_rows], 1),
        (c.at[:, mine_b], c.at[:, their_b], cs.at[mine_rows], 2),
    ]

    def own_copy(move):
        return pltpu.make_async_copy(move[0], move[2], own_sem.at[move[3]])

    def pair_copy(move):
        return pltpu.make_async_remote_copy(
            src_ref=move[1], dst_ref=move[2],
            send_sem=pair_send.at[move[3]], recv_sem=pair_recv.at[move[3]],
            device_id={"ctx": partner}, device_id_type=MESH,
        )

    held = bias.shape[0]
    lane = lax.broadcasted_iota(jnp.int32, (8, par.shape[1]), 1)
    line = lax.broadcasted_iota(jnp.int32, (8, par.shape[1]), 0)
    tile = jnp.zeros(par.shape, F32)
    for k in range(held):
        here = lane == me * held + k
        tile = jnp.where(here & (line == 0), bias[k], tile)
        tile = jnp.where(here & (line == 1), log_rate[k], tile)
    par[...] = tile

    for move in small_moves:
        own_copy(move).start()

    def start_own(q, carry):
        for move in moves_of(q):
            own_copy(move).start()
        return carry

    lax.fori_loop(0, steps, start_own, 0)

    barrier = pltpu.get_barrier_semaphore()

    def greet(d, carry):
        pl.semaphore_signal(
            barrier, inc=1, device_id={"ctx": lax.rem(me + d, count)}, device_id_type=MESH
        )
        return carry

    def greet_dp(d, carry):
        pl.semaphore_signal(
            barrier, inc=1, device_id={"dp": lax.rem(me_dp + d, copies_dp)}, device_id_type=MESH
        )
        return carry

    lax.fori_loop(1, count, greet, 0)
    lax.fori_loop(1, copies_dp, greet_dp, 0)
    pl.semaphore_wait(barrier, count - 1 + copies_dp - 1)

    def par_copy(j, place):
        return pltpu.make_async_remote_copy(
            src_ref=par, dst_ref=par_r.at[place], send_sem=ps_sem.at[j], recv_sem=pr_sem.at[place],
            device_id={"ctx": 2 * j + my_half}, device_id_type=MESH,
        )

    def par_send(j, carry):
        @pl.when(2 * j + my_half != me)
        def _():
            par_copy(j, my_place).start()

        return carry

    lax.fori_loop(0, chips, par_send, 0)

    for move in small_moves:
        pair_copy(move).start()

    def start_pair(q, carry):
        for move in moves_of(q):
            pair_copy(move).start()
        return carry

    lax.fori_loop(0, steps, start_pair, 0)

    gram[...] = jnp.zeros_like(gram)
    row[...] = jnp.zeros_like(row)
    col[...] = jnp.zeros_like(col)
    dcs[...] = jnp.zeros_like(dcs)
    dbs[...] = jnp.zeros_like(dbs)
    d_skip[...] = jnp.zeros_like(d_skip)
    d_tail[...] = jnp.zeros_like(d_tail)

    @pl.when(loc == 0)
    def _():
        recv_f[...] = jnp.zeros_like(recv_f)

    @pl.when(loc == run_len - 1)
    def _():
        recv_b[...] = jnp.zeros_like(recv_b)

    @pl.when(depth == 0)
    def _():
        past_r[...] = jnp.ones_like(past_r)

    for move in small_moves:
        own_copy(move).wait()
        pair_copy(move).wait()

    i_at = lax.broadcasted_iota(jnp.int32, (rows, rows), 0)
    j_at = lax.broadcasted_iota(jnp.int32, (rows, rows), 1)
    causal = i_at >= j_at
    for at in range(groups):
        span = slice(at * STATE, (at + 1) * STATE)
        b_at = bs[:, span]
        c_at = cs[:, span]
        bt[at] = b_at.astype(F32).T.astype(BF16)
        ct[at] = c_at.astype(F32).T.astype(BF16)
        scores = jnp.where(causal, mm_nt(c_at, b_at), 0.0)
        mix[at] = scores.astype(BF16)
        mixt[at] = scores.T.astype(BF16)

    @pl.when(my_half == core)
    def _():
        par_r[my_place] = par[...]

    def par_wait(j, carry):
        @pl.when(chips * core + j != me)
        def _():
            par_copy(j, j).wait_recv()

        return carry

    lax.fori_loop(0, chips, par_wait, 0)

    def step_sizes():
        params = jnp.sum(par_r[...], axis=0)
        z = rs[...].astype(F32) + params[0:1, :]
        dt = jnp.maximum(z, 0.0) + jnp.log1p(jnp.exp(-jnp.abs(z)))
        lane = lax.broadcasted_iota(jnp.int32, (1, z.shape[1]), 1)
        own = lax.div(lane, z.shape[1] // 2) == core
        return z, dt, jnp.where(own, -jnp.exp(params[1:2, :]), 0.0)

    z, dt, rate = step_sizes()
    ones = causal.astype(F32).astype(BF16)
    cum = sum(mm(ones, part) for part in thirds(dt * rate))
    mid = cum[rows - 1 : rows, :] * 0.5
    e_hi, e_lo = halves(jnp.exp(cum - mid))
    f_hi, f_lo = halves(jnp.exp(mid - cum) * dt)
    eh[:, :LANES] = e_hi
    eh[:, LANES:] = e_lo
    fh[:, :LANES] = f_hi
    fh[:, LANES:] = f_lo
    decay[...] = jnp.broadcast_to(jnp.exp(2.0 * mid), decay.shape)
    a_hi, a_lo = halves(jnp.broadcast_to(jnp.exp(mid), (16, LANES)))
    a_both = jnp.concatenate([a_hi, a_lo], axis=1)

    def spread_of(q):
        head = lax.broadcasted_iota(jnp.int32, (LANES, WIDE), 0)
        lane = lax.broadcasted_iota(jnp.int32, (LANES, WIDE), 1)
        return (head == first_head + q * heads_w + lax.div(lane, HEADDIM)).astype(F32).astype(BF16)

    def fold(v, spread):
        high, low = halves(v)
        return mm_nt(high, spread) + mm_nt(low, spread)

    def fold_line(v, spread):
        return fold(jnp.broadcast_to(v, (16, WIDE)), spread)[0:8, :]

    def full(high, low, here):
        return high[:, here].astype(F32) + low[:, here].astype(F32)

    def dense(q):
        for move in moves_of(q):
            own_copy(move).wait()
            pair_copy(move).wait()
        at = lax.div(q, per_group)
        here = lanes_of(q)
        spread = spread_of(q)
        both = jnp.concatenate([spread, spread], axis=0)
        x_q = xs[:, here].astype(F32)
        g_q = gr[:, here].astype(F32)
        d_skip[...] += fold_line(jnp.sum(x_q * g_q, axis=0, keepdims=True), spread)
        eg_q, eg_rest = halves(mm(eh[...], both) * g_q)
        fx_q, fx_rest = halves(mm(fh[...], both) * x_q)
        eg[:, here] = eg_q
        fx[:, here] = fx_q
        eg_low[:, here] = eg_rest
        fx_low[:, here] = fx_rest
        fresh_q = mm(bt[at], fx_q) + mm(bt[at], fx_rest)
        back_q = mm(ct[at], eg_q) + mm(ct[at], eg_rest)
        scale_q = mm(a_both, both)
        for k in range(sub):
            span = slice(k * LANES, (k + 1) * LANES)
            fresh[q * sub + k] = fresh_q[:, span]
            back[q * sub + k] = back_q[:, span]
            scale[q * sub + k] = scale_q[0:8, span]

    def inner(q):
        at = lax.div(q, per_group)
        here = lanes_of(q)
        spread = spread_of(q)
        eg_q = eg[:, here]
        fx_q = fx[:, here]
        gram[at] += mm_nt(eg_q, fx_q)
        y_q = mm(mix[at], fx_q) + mm(mix[at], fx_low[:, here])
        v_q = mm(mixt[at], eg_q) + mm(mixt[at], eg_low[:, here])
        row[...] += fold(full(eg, eg_low, here) * y_q, spread)
        col[...] += fold(full(fx, fx_low, here) * v_q, spread)

    def cross():
        for at in range(groups):
            span = slice(at * STATE, (at + 1) * STATE)
            cot = jnp.where(causal, gram[at], 0.0)
            dcs[:, span] += mm(cot.astype(BF16), bs[:, span])
            dbs[:, span] += mm(cot.T.astype(BF16), cs[:, span])

    def wide(ref, q):
        return jnp.concatenate([ref[q * sub + k] for k in range(sub)], axis=1)

    def state_part(q, v, spread):
        here = lanes_of(q)
        span = pl.ds(pl.multiple_of(lax.div(q, per_group) * STATE, STATE), STATE)
        row[...] += mm_nt((full(eg, eg_low, here) * mm(cs[:, span], v)).astype(BF16), spread)
        dcs[:, span] += mm_nt(eg[:, here], v)

    def cotangent_part(q, v, spread):
        here = lanes_of(q)
        span = pl.ds(pl.multiple_of(lax.div(q, per_group) * STATE, STATE), STATE)
        col[...] += mm_nt((full(fx, fx_low, here) * mm(bs[:, span], v)).astype(BF16), spread)
        dbs[:, span] += mm_nt(fx[:, here], v)

    def outer_near(q):
        by = wide(scale, q)[0:1, :]
        spread = spread_of(q)

        @pl.when(side == 0)
        def _():
            v = (by * unpack(wide(recv_f, q))).astype(BF16)
            kept[q] = v
            state_part(q, v, spread)

        @pl.when(side == 1)
        def _():
            v = (by * unpack(wide(recv_b, q))).astype(BF16)
            kept[q] = v
            cotangent_part(q, v, spread)

    def outer_far(q):
        by = wide(scale, q)[0:1, :]
        spread = spread_of(q)
        both = jnp.concatenate([spread, spread], axis=0)
        past = jnp.concatenate(halves(jnp.broadcast_to(past_r[0:1, :], (16, LANES))), axis=1)
        handed = mm(past, both)[0:1, :] * unpack(wide(recv_e, q))
        f_q = wide(fresh, q)

        def tail(s_q, t_q):
            whole = (s_q.astype(F32) + f_q) * t_q.astype(F32)
            d_tail[...] += fold_line(jnp.sum(whole, axis=0, keepdims=True), spread)

        @pl.when(side == 1)
        def _():
            v = (by * (unpack(wide(recv_f, q)) + handed)).astype(BF16)
            tail(v, kept[q])
            state_part(q, v, spread)

        @pl.when(side == 0)
        def _():
            v = (by * (unpack(wide(recv_b, q)) + handed)).astype(BF16)
            tail(kept[q], v)
            cotangent_part(q, v, spread)

    def copy_to(src, dst, send_sem, recv_sem, other):
        return pltpu.make_async_remote_copy(
            src_ref=src, dst_ref=dst, send_sem=send_sem, recv_sem=recv_sem,
            device_id={"ctx": other}, device_id_type=MESH,
        )

    def up(k):
        return copy_to(send_f.at[k], recv_f.at[k], fs_sem.at[k], fr_sem.at[k], chip_at(side, loc + 1))

    def down(k):
        return copy_to(send_b.at[k], recv_b.at[k], bs_sem.at[k], br_sem.at[k], chip_at(side, loc - 1))

    def over_f(k):
        return copy_to(send_f.at[k], recv_e.at[k], fs_sem.at[k], er_sem.at[k], chip_at(1 - side, loc))

    def over_b(k):
        return copy_to(send_b.at[k], recv_e.at[k], bs_sem.at[k], er_sem.at[k], chip_at(1 - side, loc))

    mid_len = run_len // 2
    last = depth == run_len - 1
    next_a = jnp.where(last, 0, jnp.where(depth < mid_len, depth + 1, depth - 1))
    has_a = ((depth < mid_len - 1) | ((depth > mid_len) & (depth < run_len - 1))) | (
        last & (run_len >= 2)
    )
    has_b = last & (run_len - 2 >= mid_len)

    def on_a(k):
        return copy_to(recv_e.at[k], recv_e.at[k], ea_sem.at[k], er_sem.at[k], at_depth(next_a))

    def on_b(k):
        return copy_to(
            recv_e.at[k], recv_e.at[k], eb_sem.at[k], er_sem.at[k], at_depth(run_len - 2)
        )

    def past_on():
        return copy_to(past_s, past_r, past_sem.at[0], past_sem.at[1], at_depth(depth + 1))

    up_next = loc < run_len - 1
    up_over = (loc == run_len - 1) & (side == 0)
    down_next = loc > 0
    down_over = (loc == 0) & (side == 1)
    from_f = 1 + loc * SKEW + jnp.where(side == 1, DELAY, 0)
    from_b = 1 + (run_len - 1 - loc) * SKEW + jnp.where(side == 0, DELAY, 0)
    hops = jnp.where(last, 0, jnp.where(depth < mid_len, depth + 1, run_len - 1 - depth))
    handed_at = 3 + run_len * SKEW
    from_e = handed_at + hops * SKEW
    far = handed_at + mid_len * SKEW
    far_from = far + sub + 2
    near_from = jnp.minimum(jnp.where(side == 0, from_f, from_b) + pieces + 1, far_from)
    early = depth <= run_len
    gap = jnp.where(early, sub, 2)
    inner_from = jnp.where(early, 2, (run_len - 1 - depth) * SKEW + pieces + 2)
    inner_from = jnp.minimum(inner_from, far + sub + pieces - steps * gap - 1)

    def slot(t, carry):
        k_f = t - from_f
        k_b = t - from_b
        k_e = t - from_e

        @pl.when((t < sub * steps) & (lax.rem(t, sub) == 0))
        def _():
            dense(lax.div(t, sub))

        @pl.when((k_f >= 0) & (k_f < pieces))
        def _():
            @pl.when(loc > 0)
            def _():
                up(k_f).wait_recv()

            @pl.when(up_next | up_over)
            def _():
                by = scale[k_f][0:1, :]
                send_f[k_f] = pack(by * (by * unpack(recv_f[k_f]) + fresh[k_f]))

            @pl.when(up_next)
            def _():
                up(k_f).start()

            @pl.when(up_over)
            def _():
                over_f(k_f).start()

        @pl.when((k_b >= 0) & (k_b < pieces))
        def _():
            @pl.when(loc < run_len - 1)
            def _():
                down(k_b).wait_recv()

            @pl.when(down_next | down_over)
            def _():
                by = scale[k_b][0:1, :]
                send_b[k_b] = pack(by * (by * unpack(recv_b[k_b]) + back[k_b]))

            @pl.when(down_next)
            def _():
                down(k_b).start()

            @pl.when(down_over)
            def _():
                over_b(k_b).start()

        @pl.when((k_e >= 0) & (k_e < pieces))
        def _():
            on_a(k_e).wait_recv()

            @pl.when(has_a)
            def _():
                on_a(k_e).start()

            @pl.when(has_b)
            def _():
                on_b(k_e).start()

        @pl.when(t == depth * SKEW + DELAY)
        def _():
            @pl.when(depth > 0)
            def _():
                past_on().wait_recv()

            @pl.when(depth < run_len - 1)
            def _():
                past_s[...] = past_r[...] * decay[...]
                past_on().start()

        k_i = t - inner_from

        @pl.when((k_i >= 0) & (k_i < steps * gap) & (lax.rem(k_i, gap) == 0))
        def _():
            inner(lax.div(k_i, gap))

        @pl.when(k_i == steps * gap)
        def _():
            cross()

        k_n = t - near_from

        @pl.when((k_n >= 0) & (k_n < steps * sub) & (lax.rem(k_n, sub) == 0))
        def _():
            outer_near(lax.div(k_n, sub))

        k_o = t - far_from

        @pl.when((k_o >= 0) & (k_o < steps * sub) & (lax.rem(k_o, sub) == 0))
        def _():
            outer_far(lax.div(k_o, sub))

        return carry

    lax.fori_loop(0, far_from + pieces, slot, 0)

    z, dt, rate = step_sizes()
    ones = (i_at <= j_at).astype(F32).astype(BF16)
    d_a = d_tail[0:1, :] + sum(mm(ones, part) for part in thirds(row[...] - col[...]))
    d_dt = col[...] / dt + rate * d_a
    d_raw = d_dt * jax.nn.sigmoid(z)
    sum_s[...] = jnp.zeros_like(sum_s)
    sum_s[0:1, :] = rate * jnp.sum(d_a * dt, axis=0, keepdims=True)
    sum_s[1:2, :] = jnp.sum(d_raw, axis=0, keepdims=True)
    sum_s[2:3, :] = d_skip[0:1, :]
    draw_s[...] = d_raw

    def sum_copy(j, place):
        return pltpu.make_async_remote_copy(
            src_ref=sum_s, dst_ref=sum_r.at[place], send_sem=ss_sem.at[j], recv_sem=sr_sem.at[place],
            device_id={"ctx": chips * core + j}, device_id_type=MESH,
        )

    def sum_send(j, carry):
        @pl.when(chips * core + j != me)
        def _():
            sum_copy(j, pos).start()

        return carry

    lax.fori_loop(0, chips, sum_send, 0)

    backs = [
        (dbs.at[their_rows], gb.at[:, mine_b]),
        (dcs.at[their_rows], gc.at[:, mine_b]),
        (draw_s.at[their_rows], draw_r),
    ]
    copies = []
    for at, (src, dst) in enumerate(backs):
        copy = pltpu.make_async_remote_copy(
            src_ref=src, dst_ref=dst, send_sem=out_send.at[at], recv_sem=out_recv.at[at],
            device_id={"ctx": partner}, device_id_type=MESH,
        )
        copy.start()
        copies.append(copy)
    own_b = pltpu.make_async_copy(dbs.at[mine_rows], gb.at[:, mine_b], own_sem.at[0])
    own_c = pltpu.make_async_copy(dcs.at[mine_rows], gc.at[:, mine_b], own_sem.at[1])
    own_b.start()
    own_c.start()

    @pl.when(my_half == core)
    def _():
        sum_r[pos] = sum_s[...]

    def sum_wait(j, carry):
        @pl.when(2 * j + my_half != me)
        def _():
            sum_copy(j, j).wait_recv()

        return carry

    lax.fori_loop(0, chips, sum_wait, 0)
    total = jnp.sum(sum_r[...], axis=0)
    all_s[...] = total

    def all_copy(d, place):
        return pltpu.make_async_remote_copy(
            src_ref=all_s, dst_ref=all_r.at[place], send_sem=as_sem.at[d], recv_sem=ar_sem.at[place],
            device_id={"dp": lax.rem(me_dp + d, copies_dp)}, device_id_type=MESH,
        )

    def all_send(d, carry):
        all_copy(d, d).start()
        return carry

    def all_wait(d, carry):
        all_copy(d, d).wait()
        return carry

    lax.fori_loop(1, copies_dp, all_send, 0)

    def drain(k, carry):
        @pl.when(up_next | up_over)
        def _():
            up(k).wait_send()

        @pl.when(down_next | down_over)
        def _():
            down(k).wait_send()

        @pl.when(has_a)
        def _():
            on_a(k).wait_send()

        @pl.when(has_b)
        def _():
            on_b(k).wait_send()

        return carry

    lax.fori_loop(0, pieces, drain, 0)

    def drain_small(j, carry):
        @pl.when(2 * j + my_half != me)
        def _():
            par_copy(j, my_place).wait_send()

        @pl.when(chips * core + j != me)
        def _():
            sum_copy(j, pos).wait_send()

        return carry

    lax.fori_loop(0, chips, drain_small, 0)

    @pl.when(depth < run_len - 1)
    def _():
        past_on().wait_send()

    for copy in copies:
        copy.wait()
    gs_v[...] = (draw_s[mine_rows, :] + draw_r[...]).astype(BF16)
    own_s = pltpu.make_async_copy(gs_v, gs, own_sem.at[2])
    own_s.start()
    lax.fori_loop(1, copies_dp, all_wait, 0)
    all_r[0] = total
    own_b.wait()
    own_c.wait()
    own_s.wait()
    heads = total.shape[1]
    head = lax.broadcasted_iota(jnp.int32, (heads, heads), 0)
    lane = lax.broadcasted_iota(jnp.int32, (heads, heads), 1)
    pick = ((head == me * held + lane) & (lane < held)).astype(F32).astype(BF16)
    gp[...] = sum(mm(part, pick) for part in thirds(jnp.sum(all_r[...], axis=0)))


def finish(gb, gc, gs, gp, gb_out, gc_out, gs_out, decay_out, bias_out, skip_out):
    gb_out[...] = gb[...]
    gc_out[...] = gc[...]
    gs_out[...] = gs[...]
    span = decay_out.shape[1]
    decay_out[...] = gp[0:1, :span]
    bias_out[...] = gp[1:2, :span]
    skip_out[...] = gp[2:3, :span]


def run(x, g, b, c, raw, bias, log_rate, chips, copies_dp):
    tok, wide = x.shape
    half = wide // 2
    cols = b.shape[1] // 2
    groups = cols // STATE
    rows = 2 * tok
    pieces = half // LANES
    heads = raw.shape[1]
    steps = half // WIDE
    anywhere = pl.BlockSpec(memory_space=pl.ANY)
    inside = pl.BlockSpec(memory_space=pltpu.VMEM)
    scalars = pl.BlockSpec(memory_space=pltpu.SMEM)
    state16 = pltpu.VMEM((pieces, STATE, LANES), BF16)
    state32 = pltpu.VMEM((pieces, STATE, LANES), F32)
    wide16 = pltpu.VMEM((rows, half), BF16)
    tile = pltpu.VMEM((8, heads), F32)
    dma = pltpu.SemaphoreType.DMA
    moves = 3 + 2 * steps
    parts = pl.pallas_call(
        partial(kernel, chips, copies_dp),
        out_shape=(
            jax.ShapeDtypeStruct((tok, 2 * cols), F32),
            jax.ShapeDtypeStruct((tok, 2 * cols), F32),
            jax.ShapeDtypeStruct((tok, heads), BF16),
            jax.ShapeDtypeStruct((8, heads), F32),
        ),
        in_specs=[anywhere] * 5 + [scalars] * 2,
        out_specs=(anywhere,) * 3 + (inside,),
        scratch_shapes=[
            wide16, wide16,
            pltpu.VMEM((rows, cols), BF16), pltpu.VMEM((rows, cols), BF16),
            pltpu.VMEM((rows, heads), BF16),
            pltpu.VMEM((rows, 2 * LANES), BF16), pltpu.VMEM((rows, 2 * LANES), BF16),
            wide16, wide16, wide16, wide16,
            state32, state32, state16, state16, state16, state16, state16,
            pltpu.VMEM((steps, STATE, WIDE), BF16),
            pltpu.VMEM((pieces, 8, LANES), F32),
            tile, tile, tile,
            pltpu.VMEM((groups, rows, rows), F32),
            pltpu.VMEM((groups, rows, rows), BF16), pltpu.VMEM((groups, rows, rows), BF16),
            pltpu.VMEM((groups, STATE, rows), BF16), pltpu.VMEM((groups, STATE, rows), BF16),
            pltpu.VMEM((rows, LANES), F32), pltpu.VMEM((rows, LANES), F32),
            pltpu.VMEM((rows, cols), F32), pltpu.VMEM((rows, cols), F32),
            tile, tile,
            pltpu.VMEM((rows, heads), F32), pltpu.VMEM((tok, heads), F32),
            pltpu.VMEM((tok, heads), BF16),
            tile, pltpu.VMEM((chips, 8, heads), F32),
            tile, pltpu.VMEM((chips, 8, heads), F32),
            tile, pltpu.VMEM((copies_dp, 8, heads), F32),
            dma((moves,)), dma((moves,)), dma((moves,)),
            dma((pieces,)), dma((pieces,)), dma((pieces,)), dma((pieces,)),
            dma((pieces,)), dma((pieces,)), dma((pieces,)),
            dma((2,)),
            dma((3,)), dma((3,)),
            dma((chips,)), dma((chips,)), dma((chips,)), dma((chips,)),
            dma((copies_dp,)), dma((copies_dp,)),
        ],
        compiler_params=pltpu.CompilerParams(
            collective_id=0, has_side_effects=True, vmem_limit_bytes=60 * 1024 * 1024
        ),
        name="scan_backward",
    )(x, g, b, c, raw, bias, log_rate)
    line = jax.ShapeDtypeStruct((1, bias.shape[0]), F32)
    return pl.pallas_call(
        finish,
        out_shape=tuple(jax.ShapeDtypeStruct(v.shape, v.dtype) for v in parts[:3]) + (line,) * 3,
        in_specs=[inside] * 4,
        out_specs=(inside,) * 6,
        compiler_params=pltpu.CompilerParams(vmem_limit_bytes=60 * 1024 * 1024),
        name="results",
    )(*parts)


def local(x_tokens, grad_out, step_raw, step_bias, decay_log, b_proj, c_proj):
    gb, gc, gs, decay, bias, skip = run(
        x_tokens[0], grad_out[0], b_proj[0], c_proj[0], step_raw[0], step_bias, decay_log,
        lax.axis_size("ctx") // 2, lax.axis_size("dp"),
    )
    return (gb[None], gc[None], gs[None], decay[0], bias[0], skip[0])


def solution(mesh):
    tokens = P("dp", "ctx", None)
    return jax.shard_map(
        local,
        mesh=mesh,
        in_specs=(tokens, tokens, tokens, P("ctx"), P("ctx"), tokens, tokens),
        out_specs=(tokens, tokens, tokens, P("ctx"), P("ctx"), P("ctx")),
        check_vma=False,
    )
```
